32 devices in a mesh: rep: 2 (over y), srv: 2 (over x), tp: 8 (over z, core).
Axes of the slice: x: 2, y: 2, z: 4, core: 2. Of those that a mesh axis runs over, the one named last changes fastest.
Arguments:
- tokens: bfloat16 [2, 160, 8192], P(None, ('rep', 'srv'), 'tp'), parts along dimension 1, may hold values from -6 to 6
- input_norm_gain: bfloat16 [8192], P('tp'), may hold values from 0.25 to 1.75
- query_weight: bfloat16 [8192, 8192], P(None, 'tp'), may hold values from -0.0625 to 0.0625
- key_weight: bfloat16 [8192, 1024], P(None, 'tp'), may hold values from -0.0625 to 0.0625
- value_weight: bfloat16 [8192, 1024], P(None, 'tp'), may hold values from -0.0625 to 0.0625
- output_weight: bfloat16 [8192, 8192], P('tp'), may hold values from -0.0625 to 0.0625
- adapter_down_maps: bfloat16 [8, 8192, 128], P('srv', 'tp'), may hold values from -0.0625 to 0.0625
- adapter_query_up: bfloat16 [8, 64, 8192], P('srv', None, 'tp'), may hold values from -0.75 to 0.75
- adapter_value_up: bfloat16 [8, 64, 1024], P('srv', None, 'tp'), may hold values from -0.75 to 0.75
- key_value_cache: bfloat16 [160, 128, 2, 1024], P(('rep', 'srv', 'tp')), parts along dimension 0, may hold values from -480 to 480, as said below
- cached_length: int32 [160], P(('rep', 'srv', 'tp')), parts along dimension 0, may hold values from 1 to 128, as said below
- request_adapter_entry: int32 [160], P(('rep', 'srv')), parts along dimension 0, may hold values from 0 to 2
- group_adapter_ids: int32 [2, 3], replicated, may hold values from 0 to 7, as said below
- adapter_slot_table: int32 [8], replicated, may hold values from 0 to 7, as said below
Outputs:
- mixed: bfloat16 [2, 160, 8192], P(None, ('rep', 'srv'), 'tp'), parts along dimension 1
The draws below stay inside these ranges and needn't reach their ends.
There are 2 independent parts, one for each index of `rep`. The reference program is written for one: setup_inputs(seed, part) draws one part's arguments, and reference() takes and returns one part's arrays. A program takes and returns all parts, laid end to end along the dimension named above; an argument that names none is the same for every part. Nothing has to cross between parts.
Inputs may be any that keep to these rules, and one draw needn't show every extreme that they name: `request_adapter_entry`: index into the request's group's row of group_adapter_ids. `group_adapter_ids`: each row lists 3 different adapter ids. Adapter a is stored at slot adapter_slot_table[a] of adapter_down_maps, adapter_query_up and adapter_value_up; every slot once. The new tokens of a request sit at positions cached_length and cached_length + 1. `key_value_cache`: keys are stored with the rotary embedding already applied.
All inputs are finite; a program needn't handle non-finite values.
Results may differ from the reference program's by a relative error of at most 0.011.
Values may be sent and summed in bfloat16 or wider, within the bound.
A program may use at most 128 MiB of HBM per device.

```python
import math
import jax
import jax.numpy as jnp
import numpy as np
from jax import lax

MODEL_WIDTH = 8192
KV_HEADS = 8
HEAD = 128
ADAPTER_RANK = 64
STEPS = 2
REQ_DEV = 5
CACHE = 128
NEED = 3
KEY_HEAD_WIDTH = 1024
REQ = 40
REQUESTS = 80
GROUPS = 2
ADAPTER_TOTAL = 8


def draw_key_value_cache(key, part):
    key = jax.random.fold_in(key, 11)
    base_key = jax.random.fold_in(key, 0)
    shape = (REQUESTS, CACHE, 2, KEY_HEAD_WIDTH)
    cache = jax.random.normal(base_key, shape, jnp.float32)
    return cache.astype(jnp.bfloat16)


def draw_cached_length(key, part):
    key = jax.random.fold_in(key, 23)
    first, second = jax.random.split(key)
    lengths = jax.random.randint(first, (REQUESTS,), 1, CACHE + 1)
    spot = jax.random.randint(second, (), 0, REQUESTS)
    return lengths.at[spot].set(CACHE).astype(jnp.int32)


def draw_group_adapter_ids(key, part):
    key = jax.random.fold_in(key, 37)

    def one_row(row_key):
        return jax.random.permutation(row_key, ADAPTER_TOTAL)[:NEED]
    return jax.vmap(one_row)(jax.random.split(key, GROUPS)).astype(jnp.int32)


def draw_adapter_slot_table(key, part):
    key = jax.random.fold_in(key, 53)
    return jax.random.permutation(key, ADAPTER_TOTAL).astype(jnp.int32)


def plant(values, own_key, least, high):
    shape = values.shape
    spot = [jax.random.randint(jax.random.fold_in(own_key, axis), (), 0, shape[axis]) for axis in range(len(shape))]
    values = values.at[tuple(spot)].set(least)
    longest = shape.index(max(shape))
    spot[longest] = (spot[longest] + 1) % shape[longest]
    return values.at[tuple(spot)].set(high)


def levels(own_key, shape, shards, low, top_value):
    def one(dim, parts):
        heights = jax.random.uniform(jax.random.fold_in(jax.random.fold_in(own_key, 6), dim), (parts,), jnp.float32, low / len(shards), top_value / len(shards))
        return jnp.repeat(jnp.exp(heights), shape[dim] // parts).reshape((-1,) + (1,) * (len(shape) - dim - 1))

    factor_of = one(*shards[0])
    for cut in shards[1:]:
        factor_of = factor_of * one(*cut)
    return factor_of


def rank_table(count, lean):
    weights = [(1 << 20) // math.isqrt(grade ** lean) + 1 for grade in range(1, count + 1)]
    spread = 1 + sum(weights) // (1 << 30)
    return np.cumsum(np.array([max(1, weight // spread) for weight in weights]))


def ranked_ids(own_key, dims, amount, slope):
    listing = rank_table(amount, slope)
    lot = jax.random.randint(jax.random.fold_in(own_key, 1), dims, 0, int(listing[amount - 1]))
    grade = jnp.searchsorted(jnp.asarray(listing, jnp.int32), lot, side="right")
    return jax.random.permutation(jax.random.fold_in(own_key, 2), amount)[grade].astype(jnp.int32)


def bell_draw(key, dims, deviation, reach, shards=(), kind=jnp.bfloat16):
    level = levels(key, dims, shards, -0.22, 0.18) if shards else 1.0
    values = jax.random.normal(key, dims, jnp.float32) * deviation * level
    return jnp.minimum(jnp.maximum(values, -reach), reach).astype(kind)


def setup_inputs(seed: int = 0, part: int = 0) -> dict:
    keys = jax.random.split(jax.random.key(seed), 15)
    part_splits = jax.random.split(jax.random.fold_in(keys[14], part), 15)
    return {
        "tokens": bell_draw(part_splits[0], (STEPS, REQUESTS, MODEL_WIDTH), 1.0, 6.0, ((1, 2), (2, 8))),
        "input_norm_gain": jnp.clip(1.0 + 0.15 * jax.random.normal(keys[1], (MODEL_WIDTH,), jnp.float32), 0.25, 1.75).astype(jnp.bfloat16),
        "query_weight": bell_draw(keys[2], (MODEL_WIDTH, MODEL_WIDTH), MODEL_WIDTH ** -0.5, 0.0625, ((1, 8),)),
        "key_weight": bell_draw(keys[3], (MODEL_WIDTH, KEY_HEAD_WIDTH), MODEL_WIDTH ** -0.5, 0.0625, ((1, 8),)),
        "value_weight": bell_draw(keys[4], (MODEL_WIDTH, KEY_HEAD_WIDTH), MODEL_WIDTH ** -0.5, 0.0625, ((1, 8),)),
        "output_weight": bell_draw(keys[5], (MODEL_WIDTH, MODEL_WIDTH), MODEL_WIDTH ** -0.5, 0.0625, ((0, 8),)),
        "adapter_down_maps": bell_draw(keys[6], (ADAPTER_TOTAL, MODEL_WIDTH, 2 * ADAPTER_RANK), MODEL_WIDTH ** -0.5, 0.0625, ((0, 2), (1, 8))),
        "adapter_query_up": bell_draw(keys[7], (ADAPTER_TOTAL, ADAPTER_RANK, MODEL_WIDTH), ADAPTER_RANK ** -0.5, 0.75, ((0, 2), (2, 8))),
        "adapter_value_up": bell_draw(keys[8], (ADAPTER_TOTAL, ADAPTER_RANK, KEY_HEAD_WIDTH), ADAPTER_RANK ** -0.5, 0.75, ((0, 2), (2, 8))),
        "key_value_cache": draw_key_value_cache(jax.random.fold_in(jax.random.fold_in(keys[14], part), 71), part),
        "cached_length": draw_cached_length(jax.random.fold_in(jax.random.fold_in(keys[14], part), 71), part),
        "request_adapter_entry": plant(ranked_ids(part_splits[11], (REQUESTS,), NEED, 2), jax.random.fold_in(part_splits[11], 3), 0, NEED - 1).astype(jnp.int32),
        "group_adapter_ids": draw_group_adapter_ids(jax.random.fold_in(keys[14], 71), part),
        "adapter_slot_table": draw_adapter_slot_table(jax.random.fold_in(keys[14], 71), part),
    }


def normalize(values, gain):
    wide = values.astype(jnp.float32)
    scale = lax.rsqrt(lax.optimization_barrier(jnp.mean(wide * wide, axis=-1, keepdims=True)) + 1e-05)
    return (wide * scale * gain.astype(jnp.float32)).astype(jnp.bfloat16)

def rotate(block, position):
    half = block.shape[-1] // 2
    freq = jnp.exp(-(jnp.arange(half).astype(jnp.float32) * 2.0 / block.shape[-1]) * math.log(500000.0))
    angle = position.astype(jnp.float32)[:, None, None] * freq
    cosine = jnp.cos(angle)
    sine = jnp.sin(angle)
    first = block[..., :half]
    second = block[..., half:]
    return jnp.concatenate([first * cosine - second * sine, second * cosine + first * sine], axis=-1)

def attend(query, cache, length, new_keys, new_values):
    rows = query.shape[0]
    span = cache.shape[1]
    fresh = new_keys.shape[1]
    group = query.shape[1] // (KV_HEADS * HEAD)
    grouped = query.reshape(rows, KV_HEADS, group, HEAD).astype(jnp.float32)
    old_keys = cache[:, :, 0].reshape(rows, span, KV_HEADS, HEAD).astype(jnp.float32)
    old_values = cache[:, :, 1].reshape(rows, span, KV_HEADS, HEAD).astype(jnp.float32)
    keys_new = new_keys.reshape(rows, fresh, KV_HEADS, HEAD).astype(jnp.float32)
    values_new = new_values.reshape(rows, fresh, KV_HEADS, HEAD).astype(jnp.float32)
    factor = HEAD ** (-0.5)
    old_scores = jnp.einsum('rkgd,rpkd->rkgp', grouped, old_keys) * factor
    valid = jnp.arange(span)[None, :] < length[:, None]
    old_scores = jnp.where(valid[:, None, None, :], old_scores, -jnp.inf)
    new_scores = jnp.einsum('rkgd,rskd->rkgs', grouped, keys_new) * factor
    top = jnp.maximum(lax.optimization_barrier(jnp.max(old_scores, axis=-1, keepdims=True)), lax.optimization_barrier(jnp.max(new_scores, axis=-1, keepdims=True)))
    old_exp = jnp.exp(old_scores - top)
    new_exp = jnp.exp(new_scores - top)
    total = lax.optimization_barrier(jnp.sum(old_exp, axis=-1, keepdims=True)) + lax.optimization_barrier(jnp.sum(new_exp, axis=-1, keepdims=True))
    old_weight = (old_exp / total).astype(jnp.bfloat16).astype(jnp.float32)
    new_weight = (new_exp / total).astype(jnp.bfloat16).astype(jnp.float32)
    result = jnp.einsum('rkgp,rpkd->rkgd', old_weight, old_values) + jnp.einsum('rkgs,rskd->rkgd', new_weight, values_new)
    return result.reshape(rows, KV_HEADS * group * HEAD).astype(jnp.bfloat16)

def reference(tokens, input_norm_gain, query_weight, key_weight, value_weight, output_weight, adapter_down_maps, adapter_query_up, adapter_value_up, key_value_cache, cached_length, request_adapter_entry, group_adapter_ids, adapter_slot_table):
    owner_group = (jnp.arange(REQUESTS) // REQ).astype(jnp.int32)
    chosen = adapter_slot_table[group_adapter_ids[owner_group, request_adapter_entry]]
    picks = (chosen[:, None] == jnp.arange(ADAPTER_TOTAL).astype(jnp.int32)[None, :]).astype(jnp.float32)
    query_steps = []
    key_steps = []
    value_steps = []
    for step in range(STEPS):
        normed_input = normalize(tokens[step], input_norm_gain)

        def shrink(total, index_value):
            adapter_term = jnp.dot(normed_input, adapter_down_maps[index_value], preferred_element_type=jnp.float32)
            return (total + adapter_term * picks[:, index_value][:, None], None)
        shrunk, _ = lax.scan(shrink, jnp.zeros((REQUESTS, 2 * ADAPTER_RANK), jnp.float32), jnp.arange(ADAPTER_TOTAL).astype(jnp.int32))
        rank_row_values = shrunk.astype(jnp.bfloat16)

        def expand(totals, index_value):
            mask_matrix = picks[:, index_value][:, None]
            query_lift = jnp.dot(rank_row_values[:, :ADAPTER_RANK], adapter_query_up[index_value], preferred_element_type=jnp.float32) * mask_matrix
            value_lift = jnp.dot(rank_row_values[:, ADAPTER_RANK:], adapter_value_up[index_value], preferred_element_type=jnp.float32) * mask_matrix
            return ((totals[0] + query_lift, totals[1] + value_lift), None)
        start = (jnp.zeros((REQUESTS, MODEL_WIDTH), jnp.float32), jnp.zeros((REQUESTS, KEY_HEAD_WIDTH), jnp.float32))
        (query_lift, value_lift), _ = lax.scan(expand, start, jnp.arange(ADAPTER_TOTAL).astype(jnp.int32))
        query_steps.append((jnp.dot(normed_input, query_weight, preferred_element_type=jnp.float32) + query_lift).astype(jnp.bfloat16))
        key_steps.append(jnp.dot(normed_input, key_weight, preferred_element_type=jnp.float32).astype(jnp.bfloat16))
        value_steps.append((jnp.dot(normed_input, value_weight, preferred_element_type=jnp.float32) + value_lift).astype(jnp.bfloat16))
    blocks = REQUESTS // REQ_DEV
    outputs = []
    for step in range(STEPS):
        turned = rotate(query_steps[step].astype(jnp.float32).reshape(REQUESTS, -1, HEAD), cached_length + step).astype(jnp.bfloat16).reshape(REQUESTS, MODEL_WIDTH)
        fresh_keys = jnp.stack([rotate(key_steps[s].astype(jnp.float32).reshape(REQUESTS, -1, HEAD), cached_length + s).astype(jnp.bfloat16).reshape(REQUESTS, KEY_HEAD_WIDTH) for s in range(step + 1)], axis=1)
        fresh_values = jnp.stack(value_steps[:step + 1], axis=1)

        def one_block(pieces):
            return attend(pieces[0], pieces[1], pieces[2], pieces[3], pieces[4])
        attended = lax.map(one_block, (turned.reshape(blocks, REQ_DEV, MODEL_WIDTH), key_value_cache.reshape(blocks, REQ_DEV, CACHE, 2, KEY_HEAD_WIDTH), cached_length.reshape(blocks, REQ_DEV), fresh_keys.reshape(blocks, REQ_DEV, step + 1, KEY_HEAD_WIDTH), fresh_values.reshape(blocks, REQ_DEV, step + 1, KEY_HEAD_WIDTH)))
        attended = attended.reshape(REQUESTS, MODEL_WIDTH)
        projected = jnp.dot(attended, output_weight, preferred_element_type=jnp.float32)
        outputs.append((tokens[step].astype(jnp.float32) + projected).astype(jnp.bfloat16))
    return jnp.stack(outputs)
```

```python
import functools
import math

import jax
import jax.numpy as jnp
from jax import lax
from jax.experimental import pallas as pl
from jax.experimental.pallas import tpu as pltpu
from jax.sharding import PartitionSpec as P

KV_HEADS = 8
HEAD = 128
STEPS = 2
CORES = 2
MESH = pl.DeviceIdType.MESH
F32 = jnp.float32
BF16 = jnp.bfloat16


def normalize(values, gain):
    wide = values.astype(jnp.float32)
    scale = lax.rsqrt(jnp.mean(wide * wide, axis=-1, keepdims=True) + 1e-05)
    return (wide * scale * gain.astype(jnp.float32)).astype(jnp.bfloat16)


def rotate(block, position):
    half = block.shape[-1] // 2
    freq = jnp.exp(
        -(jnp.arange(half).astype(jnp.float32) * 2.0 / block.shape[-1]) * math.log(500000.0)
    )
    angle = position.astype(jnp.float32)[:, None, None] * freq
    cosine = jnp.cos(angle)
    sine = jnp.sin(angle)
    first = block[..., :half]
    second = block[..., half:]
    return jnp.concatenate(
        [first * cosine - second * sine, second * cosine + first * sine], axis=-1
    )


def attend(query, cache, length, new_keys, new_values):
    rows = query.shape[0]
    span = cache.shape[1]
    fresh = new_keys.shape[1]
    group = query.shape[1] // (KV_HEADS * HEAD)
    grouped = query.reshape(rows, KV_HEADS, group, HEAD)
    old_keys = cache[:, :, 0].reshape(rows, span, KV_HEADS, HEAD)
    old_values = cache[:, :, 1].reshape(rows, span, KV_HEADS, HEAD)
    keys_new = new_keys.reshape(rows, fresh, KV_HEADS, HEAD)
    values_new = new_values.reshape(rows, fresh, KV_HEADS, HEAD)
    factor = HEAD ** (-0.5)
    old_scores = (
        jnp.einsum("rkgd,rpkd->rkgp", grouped, old_keys, preferred_element_type=jnp.float32)
        * factor
    )
    valid = jnp.arange(span)[None, :] < length[:, None]
    old_scores = jnp.where(valid[:, None, None, :], old_scores, -jnp.inf)
    new_scores = (
        jnp.einsum("rkgd,rskd->rkgs", grouped, keys_new, preferred_element_type=jnp.float32)
        * factor
    )
    top = jnp.maximum(
        jnp.max(old_scores, axis=-1, keepdims=True), jnp.max(new_scores, axis=-1, keepdims=True)
    )
    old_exp = jnp.exp(old_scores - top)
    new_exp = jnp.exp(new_scores - top)
    total = jnp.sum(old_exp, axis=-1, keepdims=True) + jnp.sum(new_exp, axis=-1, keepdims=True)
    old_weight = (old_exp / total).astype(jnp.bfloat16)
    new_weight = (new_exp / total).astype(jnp.bfloat16)
    result = jnp.einsum(
        "rkgp,rpkd->rkgd", old_weight, old_values, preferred_element_type=jnp.float32
    )
    result = result + jnp.einsum(
        "rkgs,rskd->rkgd", new_weight, values_new, preferred_element_type=jnp.float32
    )
    return result.reshape(rows, KV_HEADS * group * HEAD).astype(jnp.bfloat16)


def on_device(
    tokens,
    input_norm_gain,
    query_weight,
    key_weight,
    value_weight,
    output_weight,
    adapter_down_maps,
    adapter_query_up,
    adapter_value_up,
    key_value_cache,
    cached_length,
    request_adapter_entry,
    group_adapter_ids,
    adapter_slot_table,
):
    group_index = lax.axis_index("srv")
    need = group_adapter_ids.shape[1]
    every = (
        lax.all_gather(adapter_down_maps, "srv", axis=0, tiled=True),
        lax.all_gather(adapter_query_up, "srv", axis=0, tiled=True),
        lax.all_gather(adapter_value_up, "srv", axis=0, tiled=True),
    )
    wanted = adapter_slot_table[group_adapter_ids[group_index]]
    down_need = jnp.take(every[0], wanted, axis=0)
    up_query_need = jnp.take(every[1], wanted, axis=0)
    up_value_need = jnp.take(every[2], wanted, axis=0)
    picks = (request_adapter_entry[:, None] == jnp.arange(need)[None, :]).astype(jnp.float32)
    rank = up_query_need.shape[1]

    def attend_step(step, query_rows, key_steps, value_steps):
        rows = query_rows.shape[0]
        turned = (
            rotate(query_rows.astype(jnp.float32).reshape(rows, -1, HEAD), cached_length + step)
            .astype(jnp.bfloat16)
            .reshape(rows, -1)
        )
        fresh_keys = jnp.stack(
            [
                rotate(key_steps[s].astype(jnp.float32).reshape(rows, -1, HEAD), cached_length + s)
                .astype(jnp.bfloat16)
                .reshape(rows, -1)
                for s in range(step + 1)
            ],
            axis=1,
        )
        fresh_values = jnp.stack([value_steps[s] for s in range(step + 1)], axis=1)
        return attend(turned, key_value_cache, cached_length, fresh_keys, fresh_values)

    steps_here = tokens.shape[0]
    width = tokens.shape[2]
    flat = tokens.reshape(-1, width)
    whole = lax.all_gather(flat, "tp", axis=1, tiled=True)
    gain = lax.all_gather(input_norm_gain, "tp", axis=0, tiled=True)
    normed_input = normalize(whole, gain)
    mine = lax.dynamic_slice_in_dim(normed_input, lax.axis_index("tp") * width, width, 1)
    row_picks = jnp.tile(picks, (steps_here, 1))[:, :, None]
    partial_value = jnp.einsum("md,ndk->mnk", mine, down_need, preferred_element_type=jnp.float32)
    shrunk = jnp.sum(partial_value * row_picks, axis=1)
    rank_row_values = lax.psum(shrunk, "tp").astype(jnp.bfloat16)
    query_lift = jnp.einsum(
        "mk,nkc->mnc", rank_row_values[:, :rank], up_query_need, preferred_element_type=jnp.float32
    )
    value_lift = jnp.einsum(
        "mk,nkc->mnc", rank_row_values[:, rank:], up_value_need, preferred_element_type=jnp.float32
    )
    query = (
        jnp.dot(normed_input, query_weight, preferred_element_type=jnp.float32)
        + jnp.sum(query_lift * row_picks, axis=1)
    ).astype(jnp.bfloat16)
    keys = jnp.dot(normed_input, key_weight, preferred_element_type=jnp.float32).astype(
        jnp.bfloat16
    )
    values = (
        jnp.dot(normed_input, value_weight, preferred_element_type=jnp.float32)
        + jnp.sum(value_lift * row_picks, axis=1)
    ).astype(jnp.bfloat16)

    def by_step(array):
        return array.reshape(steps_here, -1, array.shape[1])

    query, keys, values = (
        lax.all_to_all(by_step(query), "tp", split_axis=1, concat_axis=2, tiled=True),
        lax.all_to_all(by_step(keys), "tp", split_axis=1, concat_axis=2, tiled=True),
        lax.all_to_all(by_step(values), "tp", split_axis=1, concat_axis=2, tiled=True),
    )
    attended = [attend_step(step, query[step], keys, values) for step in range(STEPS)]
    finish_attended = jnp.stack(attended)
    heads = lax.all_to_all(finish_attended, "tp", split_axis=2, concat_axis=1, tiled=True)
    flat_heads = heads.reshape(-1, heads.shape[2])
    summed = lax.psum_scatter(
        lax.dot_general(
            output_weight, flat_heads, (((0,), (1,)), ((), ())), preferred_element_type=jnp.float32
        ),
        "tp",
        scatter_dimension=0,
        tiled=True,
    )
    return (tokens.astype(jnp.float32) + summed.T.reshape(tokens.shape)).astype(jnp.bfloat16)


def remote(src, dst, send, recv, device):
    return pltpu.make_async_remote_copy(
        src_ref=src,
        dst_ref=dst,
        send_sem=send,
        recv_sem=recv,
        device_id=device,
        device_id_type=MESH,
    )


def iota(shape, axis):
    return lax.broadcasted_iota(jnp.int32, shape, axis)


def dot(left, right):
    return jnp.dot(left, right, preferred_element_type=F32)


def block_kernel(
    sizes,
    tokens_ref,
    gain_ref,
    entry_ref,
    ids_ref,
    table_ref,
    length_ref,
    query_w,
    key_w,
    value_w,
    out_w,
    down_hbm,
    up_query_hbm,
    up_value_hbm,
    cache_hbm,
    out_ref,
    weight,
    wide_out,
    down,
    up,
    cache,
    pairs,
    gathered,
    xs,
    masks,
    squares,
    acc,
    half_send,
    half_recv,
    chip_sum,
    ranks,
    lift_own,
    lift_send,
    lift_recv,
    heads_send,
    heads_recv,
    turned,
    results,
    back_send,
    back_recv,
    own_part,
    sib_send,
    sib_recv,
    sum_send,
    sum_recv,
    weight_sem,
    wide_sem,
    small_sem,
    cache_sem,
    x_send,
    x_recv,
    forward_send,
    peer_send,
    peer_recv,
    square_send,
    square_recv,
    half_sem,
    chip_send,
    chip_recv,
    rank_sem,
    lift_sem,
    heads_ssem,
    heads_rsem,
    back_ssem,
    back_rsem,
    sib_ssem,
    sib_rsem,
    sum_ssem,
    sum_rsem,
):
    T, requests, here, owned, need = sizes
    chips = T // CORES
    rows = STEPS * requests
    width = tokens_ref.shape[2]
    columns = query_w.shape[1]
    group = columns // HEAD
    pad = 16
    me = lax.axis_index("tp")
    side = lax.axis_index("srv")
    z = me // CORES
    core = lax.rem(me, CORES)
    sibling = z * CORES + (1 - core)
    other = 1 - side

    def tp(index):
        return {"tp": index}

    def at_chip(k):
        return lax.rem(z + k, chips)

    peer = {"srv": other}

    def weight_copies(u):
        span = pl.ds(pl.multiple_of(u * width, width), width)
        return (
            pltpu.make_async_copy(
                query_w.at[span, :], weight.at[span, pl.ds(0, columns)], weight_sem.at[0, u]
            ),
            pltpu.make_async_copy(
                value_w.at[span, :], weight.at[span, pl.ds(columns, HEAD)], weight_sem.at[1, u]
            ),
            pltpu.make_async_copy(
                key_w.at[span, :], weight.at[span, pl.ds(columns + HEAD, HEAD)], weight_sem.at[2, u]
            ),
        )

    def wide_copy(u):
        span = pl.ds(pl.multiple_of(u * width, width), width)
        return pltpu.make_async_copy(out_w.at[:, span], wide_out.at[u], wide_sem.at[u])

    small = [pltpu.make_async_copy(down_hbm, down, small_sem.at[0])]
    for a in range(owned):
        small.append(
            pltpu.make_async_copy(
                up_query_hbm.at[a],
                up.at[a, pl.ds(0, HEAD // 2), pl.ds(0, columns)],
                small_sem.at[1 + a],
            )
        )
        small.append(
            pltpu.make_async_copy(
                up_value_hbm.at[a],
                up.at[a, pl.ds(HEAD // 2, HEAD // 2), pl.ds(columns, HEAD)],
                small_sem.at[1 + owned + a],
            )
        )
    order = [me, sibling]
    for k in range(1, chips):
        order += [at_chip(k) * CORES + core, at_chip(k) * CORES + (1 - core)]
    for copy in weight_copies(me):
        copy.start()
    for copy in small:
        copy.start()
    for u in order[1:]:
        for copy in weight_copies(u):
            copy.start()
    cache_copy = pltpu.make_async_copy(cache_hbm, cache, cache_sem)
    cache_copy.start()
    wide_order = []
    for k in list(range(1, chips)) + [0]:
        wide_order += [at_chip(k) * CORES + (1 - core), at_chip(k) * CORES + core]
    for u in wide_order:
        wide_copy(u).start()

    barrier = pltpu.get_barrier_semaphore()
    for k in range(1, T):
        pl.semaphore_signal(
            barrier, inc=1, device_id=tp(lax.rem(me + k, T)), device_id_type=MESH
        )
    pl.semaphore_signal(barrier, inc=1, device_id=peer, device_id_type=MESH)

    token = jnp.concatenate([tokens_ref[s].astype(F32) for s in range(STEPS)], axis=0)
    xs[side] = (token * gain_ref[...].astype(F32)).astype(BF16)
    square = jnp.sum(token * token, axis=1, keepdims=True)
    eye = iota((rows, HEAD), 0) == iota((rows, HEAD), 1)
    squares[me] = jnp.broadcast_to(
        jnp.sum(jnp.where(eye, square, 0.0), axis=0, keepdims=True), (8, HEAD)
    )
    request = lax.rem(iota((rows, requests), 0), requests)
    entry = jnp.sum(
        jnp.where(request == iota((rows, requests), 1), entry_ref[...], 0), axis=1, keepdims=True
    )
    slot = jnp.zeros((rows, 1), jnp.int32)
    for n in range(need):
        slot = jnp.where(entry == n, table_ref[ids_ref[side, n]], slot)
    masks[side] = jnp.where(slot == iota((rows, HEAD), 1), 1.0, 0.0).astype(BF16)

    pl.semaphore_wait(barrier, T)
    sends = []

    def send(copy):
        copy.start()
        sends.append(copy)

    mine = xs.at[side]
    send(remote(mine, gathered.at[me], x_send.at[0], x_recv.at[me], tp(sibling)))
    send(remote(mine, xs.at[side], peer_send.at[0], peer_recv.at[0], peer))
    send(remote(masks.at[side], masks.at[side], peer_send.at[1], peer_recv.at[1], peer))
    for k in range(1, chips):
        send(
            remote(
                mine, gathered.at[me], x_send.at[k], x_recv.at[me], tp(at_chip(k) * CORES + core)
            )
        )
    for k in range(1, T):
        send(
            remote(
                squares.at[me],
                squares.at[me],
                square_send.at[k],
                square_recv.at[me],
                tp(lax.rem(me + k, T)),
            )
        )

    for a in range(owned):
        up[a, pl.ds(HEAD // 2, HEAD // 2), pl.ds(0, columns)] = jnp.zeros(
            (HEAD // 2, columns), BF16
        )
        up[a, pl.ds(0, HEAD // 2), pl.ds(columns, HEAD)] = jnp.zeros((HEAD // 2, HEAD), BF16)

    def project(u, x):
        for copy in weight_copies(u):
            copy.wait()
        return dot(x, weight[pl.ds(pl.multiple_of(u * width, width), width), :])

    acc[...] = project(me, xs[side])
    for copy in small:
        copy.wait()

    def mask_of(side_rows, a):
        lane = iota((rows, HEAD), 1)
        picked = jnp.where(lane == side * owned + a, masks[side_rows].astype(F32), 0.0)
        return jnp.sum(picked, axis=1, keepdims=True)

    def shrink(side_rows):
        x = xs[side_rows]
        total = jnp.zeros((rows, HEAD), F32)
        for a in range(owned):
            total = total + dot(x, down[a]) * mask_of(side_rows, a)
        half_send[side_rows] = total.astype(BF16)

    def wait_x(u):
        remote(mine, gathered.at[u], x_send.at[0], x_recv.at[u], tp(sibling)).wait_recv()

    shrink(side)
    wait_x(sibling)
    acc[...] += project(sibling, gathered[sibling])

    remote(mine, xs.at[other], peer_send.at[0], peer_recv.at[0], peer).wait_recv()
    remote(
        masks.at[side], masks.at[other], peer_send.at[1], peer_recv.at[1], peer
    ).wait_recv()
    shrink(other)
    half = remote(
        half_send.at[1 - core], half_recv, half_sem.at[0], half_sem.at[1], tp(sibling)
    )
    send(half)

    def take(k):
        u = at_chip(k) * CORES + core
        wait_x(u)
        send(
            remote(
                gathered.at[u], gathered.at[u], forward_send.at[k], x_recv.at[u], tp(sibling)
            )
        )
        acc[...] += project(u, gathered[u])

    def take_other(k):
        u = at_chip(k) * CORES + (1 - core)
        wait_x(u)
        acc[...] += project(u, gathered[u])

    take(1)
    half.wait_recv()
    chip_total = half_send[core].astype(F32) + half_recv[...].astype(F32)
    chip_sum[z] = chip_total.astype(BF16)
    for k in range(1, chips):
        send(
            remote(
                chip_sum.at[z],
                chip_sum.at[z],
                chip_send.at[k],
                chip_recv.at[z],
                tp(at_chip(k) * CORES + core),
            )
        )
    take_other(1)
    cache_copy.wait()
    for j in range(here):
        pairs[j] = cache[j].reshape(pairs.shape[1], pairs.shape[2])
    for k in range(1, chips):
        u = at_chip(k)
        remote(
            chip_sum.at[z], chip_sum.at[u], chip_send.at[0], chip_recv.at[u], tp(sibling)
        ).wait_recv()
        chip_total = chip_total + chip_sum[u].astype(F32)
    ranks[core] = chip_total.astype(BF16)
    rank_copy = remote(
        ranks.at[core], ranks.at[core], rank_sem.at[0], rank_sem.at[1], tp(sibling)
    )
    send(rank_copy)
    take(2)
    remote(
        ranks.at[core], ranks.at[1 - core], rank_sem.at[0], rank_sem.at[1], tp(sibling)
    ).wait_recv()

    def lift(side_rows):
        rank = ranks[side_rows].astype(F32)
        total = jnp.zeros((rows, columns + HEAD), F32)
        for a in range(owned):
            total = total + dot((rank * mask_of(side_rows, a)).astype(BF16), up[a])
        return total

    lift_send[...] = lift(other).astype(BF16)
    lift_copy = remote(lift_send, lift_recv, lift_sem.at[0], lift_sem.at[1], peer)
    send(lift_copy)
    lift_own[...] = lift(side)
    take_other(2)
    for k in range(3, chips):
        take(k)
        take_other(k)
    total_square = squares[me]
    for k in range(1, T):
        u = lax.rem(me + k, T)
        remote(
            squares.at[me], squares.at[u], square_send.at[0], square_recv.at[u], tp(sibling)
        ).wait_recv()
        total_square = total_square + squares[u]
    total_column = jnp.sum(
        jnp.where(eye, jnp.broadcast_to(total_square[0:1], (rows, HEAD)), 0.0),
        axis=1,
        keepdims=True,
    )
    factor = lax.rsqrt(total_column / (T * width) + 1e-05)
    lift_copy.wait_recv()
    lifted = lift_own[...] + lift_recv[...].astype(F32)
    span = columns + HEAD
    front = ((acc[:, 0:span] + lifted) * factor).astype(BF16)
    last = (acc[:, span:] * factor).astype(BF16)

    def spread(shape, row_axis, col_axis):
        row = iota(shape, row_axis)
        u = row // pad
        i = lax.rem(row, pad)
        step = i // here
        source = step * requests + u * here + lax.rem(i, here)
        return jnp.where(
            (i < STEPS * here) & (iota(shape, col_axis) == source), 1.0, 0.0
        ).astype(BF16)

    place = spread((T * pad, rows), 0, 1)
    heads_send[:, :, 0:span] = dot(place, front).astype(BF16).reshape(T, pad, span)
    heads_send[:, :, span:] = dot(place, last).astype(BF16).reshape(T, pad, HEAD)
    for k in range(1, T):
        u = lax.rem(me + k, T)
        send(
            remote(
                heads_send.at[u], heads_recv.at[me], heads_ssem.at[k], heads_rsem.at[me], tp(u)
            )
        )
    heads_recv[me] = heads_send[me]

    row = iota((pad, HEAD), 0)
    lane = iota((pad, HEAD), 1)
    step = row // here
    index = lax.rem(row, here)
    position = jnp.zeros((pad, HEAD), jnp.int32)
    for j in range(here):
        position = jnp.where(index == j, length_ref[j], position)
    position = (position + step).astype(F32)
    freq = jnp.exp(
        -(lax.rem(lane, HEAD // 2).astype(F32) * 2.0 / HEAD) * math.log(500000.0)
    )
    angle = position * freq
    cosine = jnp.cos(angle)
    sine = jnp.where(lane < HEAD // 2, -jnp.sin(angle), jnp.sin(angle))

    def turn(block):
        wide = block.astype(F32)
        return (wide * cosine + pltpu.roll(wide, HEAD // 2, 1) * sine).astype(BF16).astype(F32)

    results[...] = jnp.zeros(results.shape, F32)
    for k in range(1, T):
        u = lax.rem(me + k, T)
        remote(
            heads_send.at[u], heads_recv.at[u], heads_ssem.at[0], heads_rsem.at[u], tp(sibling)
        ).wait_recv()
    new_keys = []
    new_values = []
    for h in range(T):
        for g in range(group):
            turned[h, pl.ds(g * pad, pad), :] = turn(
                heads_recv[h, :, g * HEAD : (g + 1) * HEAD]
            )
        new_values.append(heads_recv[h, :, columns : columns + HEAD].astype(F32))
        new_keys.append(turn(heads_recv[h, :, columns + HEAD :]))

    scale = HEAD ** (-0.5)
    per = STEPS * group
    count = pairs.shape[1]
    for j in range(here):
        queries = []
        scores = []
        fresh = [[] for _ in range(STEPS)]
        for h in range(T):
            query = jnp.concatenate(
                [
                    turned[h, pl.ds(s * here + j, group, stride=pad), :]
                    for s in range(STEPS)
                ],
                axis=0,
            )
            keys = pairs[j, :, h * HEAD : (h + 1) * HEAD]
            scores.append(
                lax.dot_general(
                    query.astype(BF16),
                    keys,
                    (((1,), (1,)), ((), ())),
                    preferred_element_type=F32,
                )
            )
            for s in range(STEPS):
                at = s * here + j
                fresh[s].append(
                    jnp.sum(query * new_keys[h][at : at + 1, :], axis=1, keepdims=True)
                )
        score = jnp.concatenate(scores, axis=0) * scale
        lanes = iota((T * per, count), 1)
        valid = (lanes < 2 * length_ref[j]) & (lax.rem(lanes, 2) == 0)
        score = jnp.where(valid, score, -1e30)
        top = jnp.max(score, axis=1, keepdims=True)
        row_step = lax.rem(iota((T * per, 1), 0), per) // group
        new_scores = []
        for s in range(STEPS):
            new = jnp.concatenate(fresh[s], axis=0) * scale
            new = jnp.where(row_step >= s, new, -1e30)
            new_scores.append(new)
            top = jnp.maximum(top, new)
        old_exp = jnp.exp(score - top)
        total = jnp.sum(old_exp, axis=1, keepdims=True)
        new_exp = [jnp.exp(new - top) for new in new_scores]
        for new in new_exp:
            total = total + new
        inverse = 1.0 / total
        shifted = pltpu.roll(old_exp * inverse, 1, 1).astype(BF16)
        new_weight = [(new * inverse).astype(BF16).astype(F32) for new in new_exp]
        for h in range(T):
            part = slice(h * per, (h + 1) * per)
            result = dot(shifted[part], pairs[j, :, h * HEAD : (h + 1) * HEAD])
            for s in range(STEPS):
                at = s * here + j
                result = result + new_weight[s][part] * new_values[h][at : at + 1, :]
            for s in range(STEPS):
                results[h, pl.ds(s * here + j, group, stride=pad), :] = result[
                    s * group : (s + 1) * group
                ]
    for h in range(T):
        for g in range(group):
            back_send[h, :, g * HEAD : (g + 1) * HEAD] = results[
                h, pl.ds(g * pad, pad), :
            ].astype(BF16)
    for k in range(1, T):
        u = lax.rem(me + k, T)
        send(
            remote(back_send.at[u], back_recv.at[me], back_ssem.at[k], back_rsem.at[me], tp(u))
        )
    back_recv[me] = back_send[me]
    collect = spread((rows, T * pad), 1, 0)
    for k in range(1, T):
        u = lax.rem(me + k, T)
        remote(
            back_send.at[u], back_recv.at[u], back_ssem.at[0], back_rsem.at[u], tp(sibling)
        ).wait_recv()
    attended = dot(collect, back_recv[...].reshape(T * pad, columns)).astype(BF16)

    def forward(k):
        u = at_chip(k) * CORES + (1 - core)
        wide_copy(u).wait()
        sib_send[k] = dot(attended, wide_out[u]).astype(BF16)
        send(remote(sib_send.at[k], sib_recv.at[k], sib_ssem.at[k], sib_rsem.at[k], tp(sibling)))
        v = at_chip(k) * CORES + core
        wide_copy(v).wait()
        own_part[k] = dot(attended, wide_out[v])

    def finish(k):
        remote(
            sib_send.at[k], sib_recv.at[k], sib_ssem.at[k], sib_rsem.at[k], tp(sibling)
        ).wait_recv()
        summed = own_part[k] + sib_recv[k].astype(F32)
        if k == 0:
            own_part[0] = summed
        else:
            sum_send[k] = summed.astype(BF16)
            send(
                remote(
                    sum_send.at[k],
                    sum_recv.at[z],
                    sum_ssem.at[k],
                    sum_rsem.at[z],
                    tp(at_chip(k) * CORES + core),
                )
            )

    turns = list(range(1, chips)) + [0]
    for i, k in enumerate(turns):
        forward(k)
        if i:
            finish(turns[i - 1])
    finish(0)
    mixed = token + own_part[0]
    for k in range(1, chips):
        u = at_chip(k)
        remote(
            sum_send.at[k], sum_recv.at[u], sum_ssem.at[k], sum_rsem.at[u], tp(sibling)
        ).wait_recv()
        mixed = mixed + sum_recv[u].astype(F32)
    for s in range(STEPS):
        out_ref[s] = mixed[s * requests : (s + 1) * requests].astype(BF16)
    for copy in sends:
        copy.wait_send()


def fused(
    tokens,
    input_norm_gain,
    query_weight,
    key_weight,
    value_weight,
    output_weight,
    adapter_down_maps,
    adapter_query_up,
    adapter_value_up,
    key_value_cache,
    cached_length,
    request_adapter_entry,
    group_adapter_ids,
    adapter_slot_table,
):
    T = lax.axis_size("tp")
    chips = T // CORES
    requests = tokens.shape[1]
    rows = STEPS * requests
    width = tokens.shape[2]
    here = cached_length.shape[0]
    owned = adapter_down_maps.shape[0]
    columns = query_weight.shape[1]
    group = columns // HEAD
    span = columns + HEAD
    pad = 16
    count = 2 * key_value_cache.shape[1]
    sizes = (T, requests, here, owned, group_adapter_ids.shape[1])
    whole = pl.BlockSpec(memory_space=pltpu.VMEM)
    scalar = pl.BlockSpec(memory_space=pltpu.SMEM)
    left = pl.BlockSpec(memory_space=pl.ANY)
    dma = pltpu.SemaphoreType.DMA
    vmem = pltpu.VMEM
    return pl.pallas_call(
        functools.partial(block_kernel, sizes),
        out_shape=jax.ShapeDtypeStruct(tokens.shape, BF16),
        in_specs=[whole] * 3 + [scalar] * 3 + [left] * 8,
        out_specs=whole,
        scratch_shapes=[
            vmem((T * width, span + HEAD), BF16),
            vmem((T, columns, width), BF16),
            vmem(adapter_down_maps.shape, BF16),
            vmem((owned, HEAD, span), BF16),
            vmem(key_value_cache.shape, BF16),
            vmem((here, count, KV_HEADS * HEAD), BF16),
            vmem((T, rows, width), BF16),
            vmem((2, rows, width), BF16),
            vmem((2, rows, HEAD), BF16),
            vmem((T, 8, HEAD), F32),
            vmem((rows, span + HEAD), F32),
            vmem((2, rows, HEAD), BF16),
            vmem((rows, HEAD), BF16),
            vmem((chips, rows, HEAD), BF16),
            vmem((2, rows, HEAD), BF16),
            vmem((rows, span), F32),
            vmem((rows, span), BF16),
            vmem((rows, span), BF16),
            vmem((T, pad, span + HEAD), BF16),
            vmem((T, pad, span + HEAD), BF16),
            vmem((T, group * pad, HEAD), F32),
            vmem((T, group * pad, HEAD), F32),
            vmem((T, pad, columns), BF16),
            vmem((T, pad, columns), BF16),
            vmem((chips, rows, width), F32),
            vmem((chips, rows, width), BF16),
            vmem((chips, rows, width), BF16),
            vmem((chips, rows, width), BF16),
            vmem((chips, rows, width), BF16),
            dma((3, T)),
            dma((T,)),
            dma((1 + 2 * owned,)),
            dma(()),
            dma((chips,)),
            dma((T,)),
            dma((chips,)),
            dma((2,)),
            dma((2,)),
            dma((T,)),
            dma((T,)),
            dma((2,)),
            dma((chips,)),
            dma((chips,)),
            dma((2,)),
            dma((2,)),
            dma((T,)),
            dma((T,)),
            dma((T,)),
            dma((T,)),
            dma((chips,)),
            dma((chips,)),
            dma((chips,)),
            dma((chips,)),
        ],
        compiler_params=pltpu.CompilerParams(
            collective_id=0, has_side_effects=True, vmem_limit_bytes=56 * 1024 * 1024
        ),
    )(
        tokens,
        input_norm_gain.reshape(1, width),
        request_adapter_entry.reshape(1, requests),
        group_adapter_ids,
        adapter_slot_table,
        cached_length,
        query_weight,
        key_weight,
        value_weight,
        output_weight,
        adapter_down_maps,
        adapter_query_up,
        adapter_value_up,
        key_value_cache,
    )


def device_program(*arrays):
    tokens, query_weight, key_weight, down = arrays[0], arrays[2], arrays[3], arrays[6]
    T = lax.axis_size("tp")
    whole_heads = (
        key_weight.shape[1] == HEAD
        and T == KV_HEADS
        and lax.axis_size("srv") == 2
        and down.shape[2] == HEAD
        and tokens.shape[2] == query_weight.shape[1]
        and (STEPS * tokens.shape[1]) % 16 == 0
        and STEPS * tokens.shape[1] <= HEAD
    )
    return fused(*arrays) if whole_heads else on_device(*arrays)


def solution(mesh):
    placed = (
        P(None, ("rep", "srv"), "tp"),
        P("tp"),
        P(None, "tp"),
        P(None, "tp"),
        P(None, "tp"),
        P("tp", None),
        P("srv", "tp", None),
        P("srv", None, "tp"),
        P("srv", None, "tp"),
        P(("rep", "srv", "tp"), None, None, None),
        P(("rep", "srv", "tp")),
        P(("rep", "srv")),
        P(),
        P(),
    )
    return jax.shard_map(
        device_program,
        mesh=mesh,
        in_specs=placed,
        out_specs=P(None, ("rep", "srv"), "tp"),
        check_vma=False,
    )
```

```python
import functools
import math

import jax
import jax.numpy as jnp
from jax import lax
from jax.experimental import pallas as pl
from jax.experimental.pallas import tpu as pltpu
from jax.sharding import PartitionSpec as P

KV_HEADS = 8
HEAD = 128
STEPS = 2
CORES = 2
MESH = pl.DeviceIdType.MESH
F32 = jnp.float32
BF16 = jnp.bfloat16


def normalize(values, gain):
    wide = values.astype(jnp.float32)
    scale = lax.rsqrt(jnp.mean(wide * wide, axis=-1, keepdims=True) + 1e-05)
    return (wide * scale * gain.astype(jnp.float32)).astype(jnp.bfloat16)


def rotate(block, position):
    half = block.shape[-1] // 2
    freq = jnp.exp(
        -(jnp.arange(half).astype(jnp.float32) * 2.0 / block.shape[-1]) * math.log(500000.0)
    )
    angle = position.astype(jnp.float32)[:, None, None] * freq
    cosine = jnp.cos(angle)
    sine = jnp.sin(angle)
    first = block[..., :half]
    second = block[..., half:]
    return jnp.concatenate(
        [first * cosine - second * sine, second * cosine + first * sine], axis=-1
    )


def attend(query, cache, length, new_keys, new_values):
    rows = query.shape[0]
    span = cache.shape[1]
    fresh = new_keys.shape[1]
    group = query.shape[1] // (KV_HEADS * HEAD)
    grouped = query.reshape(rows, KV_HEADS, group, HEAD)
    old_keys = cache[:, :, 0].reshape(rows, span, KV_HEADS, HEAD)
    old_values = cache[:, :, 1].reshape(rows, span, KV_HEADS, HEAD)
    keys_new = new_keys.reshape(rows, fresh, KV_HEADS, HEAD)
    values_new = new_values.reshape(rows, fresh, KV_HEADS, HEAD)
    factor = HEAD ** (-0.5)
    old_scores = (
        jnp.einsum("rkgd,rpkd->rkgp", grouped, old_keys, preferred_element_type=jnp.float32)
        * factor
    )
    valid = jnp.arange(span)[None, :] < length[:, None]
    old_scores = jnp.where(valid[:, None, None, :], old_scores, -jnp.inf)
    new_scores = (
        jnp.einsum("rkgd,rskd->rkgs", grouped, keys_new, preferred_element_type=jnp.float32)
        * factor
    )
    top = jnp.maximum(
        jnp.max(old_scores, axis=-1, keepdims=True), jnp.max(new_scores, axis=-1, keepdims=True)
    )
    old_exp = jnp.exp(old_scores - top)
    new_exp = jnp.exp(new_scores - top)
    total = jnp.sum(old_exp, axis=-1, keepdims=True) + jnp.sum(new_exp, axis=-1, keepdims=True)
    old_weight = (old_exp / total).astype(jnp.bfloat16)
    new_weight = (new_exp / total).astype(jnp.bfloat16)
    result = jnp.einsum(
        "rkgp,rpkd->rkgd", old_weight, old_values, preferred_element_type=jnp.float32
    )
    result = result + jnp.einsum(
        "rkgs,rskd->rkgd", new_weight, values_new, preferred_element_type=jnp.float32
    )
    return result.reshape(rows, KV_HEADS * group * HEAD).astype(jnp.bfloat16)


def on_device(
    tokens,
    input_norm_gain,
    query_weight,
    key_weight,
    value_weight,
    output_weight,
    adapter_down_maps,
    adapter_query_up,
    adapter_value_up,
    key_value_cache,
    cached_length,
    request_adapter_entry,
    group_adapter_ids,
    adapter_slot_table,
):
    group_index = lax.axis_index("srv")
    need = group_adapter_ids.shape[1]
    every = (
        lax.all_gather(adapter_down_maps, "srv", axis=0, tiled=True),
        lax.all_gather(adapter_query_up, "srv", axis=0, tiled=True),
        lax.all_gather(adapter_value_up, "srv", axis=0, tiled=True),
    )
    wanted = adapter_slot_table[group_adapter_ids[group_index]]
    down_need = jnp.take(every[0], wanted, axis=0)
    up_query_need = jnp.take(every[1], wanted, axis=0)
    up_value_need = jnp.take(every[2], wanted, axis=0)
    picks = (request_adapter_entry[:, None] == jnp.arange(need)[None, :]).astype(jnp.float32)
    rank = up_query_need.shape[1]

    def attend_step(step, query_rows, key_steps, value_steps):
        rows = query_rows.shape[0]
        turned = (
            rotate(query_rows.astype(jnp.float32).reshape(rows, -1, HEAD), cached_length + step)
            .astype(jnp.bfloat16)
            .reshape(rows, -1)
        )
        fresh_keys = jnp.stack(
            [
                rotate(key_steps[s].astype(jnp.float32).reshape(rows, -1, HEAD), cached_length + s)
                .astype(jnp.bfloat16)
                .reshape(rows, -1)
                for s in range(step + 1)
            ],
            axis=1,
        )
        fresh_values = jnp.stack([value_steps[s] for s in range(step + 1)], axis=1)
        return attend(turned, key_value_cache, cached_length, fresh_keys, fresh_values)

    steps_here = tokens.shape[0]
    width = tokens.shape[2]
    flat = tokens.reshape(-1, width)
    whole = lax.all_gather(flat, "tp", axis=1, tiled=True)
    gain = lax.all_gather(input_norm_gain, "tp", axis=0, tiled=True)
    normed_input = normalize(whole, gain)
    mine = lax.dynamic_slice_in_dim(normed_input, lax.axis_index("tp") * width, width, 1)
    row_picks = jnp.tile(picks, (steps_here, 1))[:, :, None]
    partial_value = jnp.einsum("md,ndk->mnk", mine, down_need, preferred_element_type=jnp.float32)
    shrunk = jnp.sum(partial_value * row_picks, axis=1)
    rank_row_values = lax.psum(shrunk, "tp").astype(jnp.bfloat16)
    query_lift = jnp.einsum(
        "mk,nkc->mnc", rank_row_values[:, :rank], up_query_need, preferred_element_type=jnp.float32
    )
    value_lift = jnp.einsum(
        "mk,nkc->mnc", rank_row_values[:, rank:], up_value_need, preferred_element_type=jnp.float32
    )
    query = (
        jnp.dot(normed_input, query_weight, preferred_element_type=jnp.float32)
        + jnp.sum(query_lift * row_picks, axis=1)
    ).astype(jnp.bfloat16)
    keys = jnp.dot(normed_input, key_weight, preferred_element_type=jnp.float32).astype(
        jnp.bfloat16
    )
    values = (
        jnp.dot(normed_input, value_weight, preferred_element_type=jnp.float32)
        + jnp.sum(value_lift * row_picks, axis=1)
    ).astype(jnp.bfloat16)

    def by_step(array):
        return array.reshape(steps_here, -1, array.shape[1])

    query, keys, values = (
        lax.all_to_all(by_step(query), "tp", split_axis=1, concat_axis=2, tiled=True),
        lax.all_to_all(by_step(keys), "tp", split_axis=1, concat_axis=2, tiled=True),
        lax.all_to_all(by_step(values), "tp", split_axis=1, concat_axis=2, tiled=True),
    )
    attended = [attend_step(step, query[step], keys, values) for step in range(STEPS)]
    finish_attended = jnp.stack(attended)
    heads = lax.all_to_all(finish_attended, "tp", split_axis=2, concat_axis=1, tiled=True)
    flat_heads = heads.reshape(-1, heads.shape[2])
    summed = lax.psum_scatter(
        lax.dot_general(
            output_weight, flat_heads, (((0,), (1,)), ((), ())), preferred_element_type=jnp.float32
        ),
        "tp",
        scatter_dimension=0,
        tiled=True,
    )
    return (tokens.astype(jnp.float32) + summed.T.reshape(tokens.shape)).astype(jnp.bfloat16)


def remote(src, dst, send, recv, device):
    return pltpu.make_async_remote_copy(
        src_ref=src,
        dst_ref=dst,
        send_sem=send,
        recv_sem=recv,
        device_id=device,
        device_id_type=MESH,
    )


def iota(shape, axis):
    return lax.broadcasted_iota(jnp.int32, shape, axis)


def dot(left, right):
    return jnp.dot(left, right, preferred_element_type=F32)


def block_kernel(
    sizes,
    tokens_ref,
    gain_ref,
    entry_ref,
    ids_ref,
    table_ref,
    length_ref,
    query_w,
    key_w,
    value_w,
    out_w,
    down_hbm,
    up_query_hbm,
    up_value_hbm,
    cache_hbm,
    out_ref,
    weight,
    wide_out,
    down,
    up,
    cache,
    pairs,
    gathered,
    raw,
    masks,
    stats,
    totals,
    acc,
    half_send,
    half_recv,
    chip_sum,
    ranks,
    lift_own,
    lift_send,
    lift_recv,
    heads_send,
    heads_recv,
    turned,
    results,
    back_send,
    back_recv,
    own_part,
    sib_send,
    sib_recv,
    sum_send,
    sum_recv,
    weight_sem,
    wide_sem,
    small_sem,
    cache_sem,
    x_send,
    x_recv,
    line_send,
    forward_send,
    peer_send,
    peer_recv,
    stat_send,
    stat_recv,
    half_sem,
    chip_send,
    chip_recv,
    rank_sem,
    lift_sem,
    heads_ssem,
    heads_rsem,
    back_ssem,
    back_rsem,
    sib_ssem,
    sib_rsem,
    sum_ssem,
    sum_rsem,
):
    T, requests, here, owned, need = sizes
    chips = T // CORES
    rows = STEPS * requests
    width = tokens_ref.shape[2]
    columns = query_w.shape[1]
    group = columns // HEAD
    pad = 16
    me = lax.axis_index("tp")
    side = lax.axis_index("srv")
    z = me // CORES
    core = lax.rem(me, CORES)
    sibling = z * CORES + (1 - core)
    other = 1 - side

    def tp(index):
        return {"tp": index}

    def at_chip(k):
        return lax.rem(z + k, chips)

    peer = {"srv": other}
    last = chips - 1

    def pick(lists, i):
        value = lists[0][i]
        for at in range(1, chips):
            value = jnp.where(z == at, lists[at][i], value)
        return value

    near = [
        sorted((v for v in range(chips) if v != at), key=lambda v: (abs(v - at), v))
        for at in range(chips)
    ]

    def ready(at, v):
        if v == at:
            return 4 * chips
        return at + last - v if v > at else last - at + v

    onward = [
        sorted(range(chips), key=lambda v: (ready(at, v), abs(v - at))) for at in range(chips)
    ]
    sources = [pick(near, i) for i in range(last)]
    targets = [pick(onward, i) for i in range(chips)]

    def weight_copies(u):
        span = pl.ds(pl.multiple_of(u * width, width), width)
        return (
            pltpu.make_async_copy(
                query_w.at[span, :], weight.at[span, pl.ds(0, columns)], weight_sem.at[0, u]
            ),
            pltpu.make_async_copy(
                value_w.at[span, :], weight.at[span, pl.ds(columns, HEAD)], weight_sem.at[1, u]
            ),
            pltpu.make_async_copy(
                key_w.at[span, :], weight.at[span, pl.ds(columns + HEAD, HEAD)], weight_sem.at[2, u]
            ),
        )

    def wide_copy(u):
        span = pl.ds(pl.multiple_of(u * width, width), width)
        return pltpu.make_async_copy(out_w.at[:, span], wide_out.at[u], wide_sem.at[u])

    small = [pltpu.make_async_copy(down_hbm, down, small_sem.at[0])]
    for a in range(owned):
        small.append(
            pltpu.make_async_copy(
                up_query_hbm.at[a],
                up.at[a, pl.ds(0, HEAD // 2), pl.ds(0, columns)],
                small_sem.at[1 + a],
            )
        )
        small.append(
            pltpu.make_async_copy(
                up_value_hbm.at[a],
                up.at[a, pl.ds(HEAD // 2, HEAD // 2), pl.ds(columns, HEAD)],
                small_sem.at[1 + owned + a],
            )
        )
    order = [me, sibling]
    for v in sources:
        order += [v * CORES + core, v * CORES + (1 - core)]
    for copy in weight_copies(me):
        copy.start()
    for copy in small:
        copy.start()
    cache_copy = pltpu.make_async_copy(cache_hbm, cache, cache_sem)
    cache_copy.start()
    for u in order[1:]:
        for copy in weight_copies(u):
            copy.start()
    wide_order = []
    for v in targets:
        wide_order += [v * CORES + (1 - core), v * CORES + core]
    for u in wide_order:
        wide_copy(u).start()

    barrier = pltpu.get_barrier_semaphore()
    for k in range(1, T):
        pl.semaphore_signal(
            barrier, inc=1, device_id=tp(lax.rem(me + k, T)), device_id_type=MESH
        )
    pl.semaphore_signal(barrier, inc=1, device_id=peer, device_id_type=MESH)

    token = jnp.concatenate([tokens_ref[s].astype(F32) for s in range(STEPS)], axis=0)
    raw[side] = token.astype(BF16)
    square = jnp.sum(token * token, axis=1, keepdims=True)
    eye = iota((rows, HEAD), 0) == iota((rows, HEAD), 1)
    square = jnp.sum(jnp.where(eye, square, 0.0), axis=0, keepdims=True)
    high = square.astype(BF16).astype(F32)
    middle = (square - high).astype(BF16).astype(F32)
    low = square - high - middle
    gain = gain_ref[...].astype(F32)
    gain_rows = width // HEAD
    stats[me] = jnp.concatenate(
        [gain[:, i * HEAD : (i + 1) * HEAD] for i in range(gain_rows)]
        + [high, middle, low, jnp.zeros((16 - 3 - gain_rows, HEAD), F32)],
        axis=0,
    ).astype(BF16)
    request = lax.rem(iota((rows, requests), 0), requests)
    entry = jnp.sum(
        jnp.where(request == iota((rows, requests), 1), entry_ref[...], 0), axis=1, keepdims=True
    )
    slot = jnp.zeros((rows, 1), jnp.int32)
    for n in range(need):
        slot = jnp.where(entry == n, table_ref[ids_ref[side, n]], slot)
    masks[side] = jnp.where(slot == iota((rows, HEAD), 1), 1.0, 0.0).astype(BF16)

    pl.semaphore_wait(barrier, T)
    sends = []

    def send(copy):
        copy.start()
        sends.append(copy)

    mine = raw.at[side]
    for k in range(1, T):
        send(
            remote(
                stats.at[me], stats.at[me], stat_send.at[k], stat_recv.at[me], tp(lax.rem(me + k, T))
            )
        )

    def conditional(condition, copy):
        @pl.when(condition)
        def _():
            copy.start()

        maybe.append((condition, copy))

    maybe = []

    def along(u, block, right, left, i):
        for condition, step, s in ((right, 1, 0), (left, -1, 1)):
            conditional(
                condition,
                remote(
                    block, gathered.at[u], line_send.at[i, s], x_recv.at[u], tp(me + step * CORES)
                ),
            )

    along(me, mine, z < last, z > 0, 0)
    send(remote(masks.at[side], masks.at[side], peer_send.at[1], peer_recv.at[1], peer))
    send(remote(mine, raw.at[side], peer_send.at[0], peer_recv.at[0], peer))
    send(remote(mine, gathered.at[me], x_send, x_recv.at[me], tp(sibling)))

    for a in range(owned):
        up[a, pl.ds(HEAD // 2, HEAD // 2), pl.ds(0, columns)] = jnp.zeros(
            (HEAD // 2, columns), BF16
        )
        up[a, pl.ds(0, HEAD // 2), pl.ds(columns, HEAD)] = jnp.zeros((HEAD // 2, HEAD), BF16)

    def project(u, x):
        for copy in weight_copies(u):
            copy.wait()
        return dot(x, weight[pl.ds(pl.multiple_of(u * width, width), width), :])

    cache_copy.wait()
    for j in range(here):
        pairs[j] = cache[j].reshape(pairs.shape[1], pairs.shape[2])

    def squares_of(u):
        block = stats[u].astype(F32)
        top_row = gain_rows
        return (
            block[top_row : top_row + 1]
            + block[top_row + 1 : top_row + 2]
            + block[top_row + 2 : top_row + 3]
        )

    def gain_of(u):
        block = stats[u].astype(F32)
        return jnp.concatenate([block[i : i + 1] for i in range(gain_rows)], axis=1)

    def factor_of(total):
        column = jnp.sum(
            jnp.where(eye, jnp.broadcast_to(total, (rows, HEAD)), 0.0), axis=1, keepdims=True
        )
        return lax.rsqrt(column / (T * width) + 1e-05)

    total_square = squares_of(me)
    for k in range(1, T):
        u = lax.rem(me + k, T)
        remote(
            stats.at[me], stats.at[u], stat_send.at[0], stat_recv.at[u], tp(sibling)
        ).wait_recv()
        total_square = total_square + squares_of(u)
    totals[side] = jnp.broadcast_to(total_square, (8, HEAD))
    send(remote(totals.at[side], totals.at[side], peer_send.at[2], peer_recv.at[2], peer))
    factor = factor_of(total_square)

    def normed(block, row_factor, u):
        return (block.astype(F32) * row_factor * gain_of(u)).astype(BF16)

    normed_mine = normed(raw[side], factor, me)
    acc[...] = project(me, normed_mine)
    for copy in small:
        copy.wait()

    def mask_of(side_rows, a):
        lane = iota((rows, HEAD), 1)
        picked = jnp.where(lane == side * owned + a, masks[side_rows].astype(F32), 0.0)
        return jnp.sum(picked, axis=1, keepdims=True)

    def shrink(side_rows, x):
        total = jnp.zeros((rows, HEAD), F32)
        for a in range(owned):
            total = total + dot(x, down[a]) * mask_of(side_rows, a)
        half_send[side_rows] = total

    def wait_x(u):
        remote(mine, gathered.at[u], x_send, x_recv.at[u], tp(sibling)).wait_recv()

    def add_block(u):
        acc[...] += project(u, normed(gathered[u], factor, u))

    def arrive(i):
        v = sources[i]
        u = v * CORES + core
        wait_x(u)
        along(u, gathered.at[u], (v < z) & (z < last), (v > z) & (z > 0), i + 1)
        send(
            remote(gathered.at[u], gathered.at[u], forward_send.at[i], x_recv.at[u], tp(sibling))
        )

    def add_same(i):
        add_block(sources[i] * CORES + core)

    def add_other(i):
        u = sources[i] * CORES + (1 - core)
        wait_x(u)
        add_block(u)

    shrink(side, normed_mine)
    arrive(0)
    remote(masks.at[side], masks.at[other], peer_send.at[1], peer_recv.at[1], peer).wait_recv()
    remote(totals.at[side], totals.at[other], peer_send.at[2], peer_recv.at[2], peer).wait_recv()
    remote(mine, raw.at[other], peer_send.at[0], peer_recv.at[0], peer).wait_recv()
    shrink(other, normed(raw[other], factor_of(totals[other][0:1]), me))
    half = remote(
        half_send.at[1 - core], half_recv, half_sem.at[0], half_sem.at[1], tp(sibling)
    )
    send(half)
    wait_x(sibling)
    add_block(sibling)
    half.wait_recv()
    chip_total = half_send[core] + half_recv[...]
    chip_sum[z] = chip_total.astype(chip_sum.dtype)
    for k in range(1, chips):
        send(
            remote(
                chip_sum.at[z],
                chip_sum.at[z],
                chip_send.at[k],
                chip_recv.at[z],
                tp(at_chip(k) * CORES + core),
            )
        )
    add_same(0)
    arrive(1)
    add_other(0)
    add_same(1)
    for k in range(1, chips):
        v = at_chip(k)
        remote(
            chip_sum.at[z], chip_sum.at[v], chip_send.at[0], chip_recv.at[v], tp(sibling)
        ).wait_recv()
        chip_total = chip_total + chip_sum[v].astype(F32)
    ranks[core] = chip_total.astype(BF16)
    rank_copy = remote(
        ranks.at[core], ranks.at[core], rank_sem.at[0], rank_sem.at[1], tp(sibling)
    )
    send(rank_copy)
    add_other(1)
    remote(
        ranks.at[core], ranks.at[1 - core], rank_sem.at[0], rank_sem.at[1], tp(sibling)
    ).wait_recv()

    def lift(side_rows):
        rank = ranks[side_rows].astype(F32)
        total = jnp.zeros((rows, columns + HEAD), F32)
        for a in range(owned):
            total = total + dot((rank * mask_of(side_rows, a)).astype(BF16), up[a])
        return total

    lift_send[...] = lift(other).astype(BF16)
    lift_copy = remote(lift_send, lift_recv, lift_sem.at[0], lift_sem.at[1], peer)
    send(lift_copy)
    lift_own[...] = lift(side)
    for i in range(2, last):
        arrive(i)
        add_same(i)
        add_other(i)
    lift_copy.wait_recv()
    span = columns + HEAD
    front = (acc[:, 0:span] + lift_own[...] + lift_recv[...].astype(F32)).astype(BF16)
    key_block = acc[:, span:].astype(BF16)

    def spread(shape, row_axis, col_axis):
        row = iota(shape, row_axis)
        u = row // pad
        i = lax.rem(row, pad)
        step = i // here
        source = step * requests + u * here + lax.rem(i, here)
        return jnp.where(
            (i < STEPS * here) & (iota(shape, col_axis) == source), 1.0, 0.0
        ).astype(BF16)

    place = spread((T * pad, rows), 0, 1)
    heads_send[:, :, 0:span] = dot(place, front).astype(BF16).reshape(T, pad, span)
    heads_send[:, :, span:] = dot(place, key_block).astype(BF16).reshape(T, pad, HEAD)
    for k in range(1, T):
        u = lax.rem(me + k, T)
        send(
            remote(
                heads_send.at[u], heads_recv.at[me], heads_ssem.at[k], heads_rsem.at[me], tp(u)
            )
        )
    heads_recv[me] = heads_send[me]

    row = iota((pad, HEAD), 0)
    lane = iota((pad, HEAD), 1)
    step = row // here
    index = lax.rem(row, here)
    position = jnp.zeros((pad, HEAD), jnp.int32)
    for j in range(here):
        position = jnp.where(index == j, length_ref[j], position)
    position = (position + step).astype(F32)
    freq = jnp.exp(
        -(lax.rem(lane, HEAD // 2).astype(F32) * 2.0 / HEAD) * math.log(500000.0)
    )
    angle = position * freq
    cosine = jnp.cos(angle)
    sine = jnp.where(lane < HEAD // 2, -jnp.sin(angle), jnp.sin(angle))

    def turn(block):
        wide = block.astype(F32)
        return (wide * cosine + pltpu.roll(wide, HEAD // 2, 1) * sine).astype(BF16).astype(F32)

    results[...] = jnp.zeros(results.shape, F32)
    for k in range(1, T):
        u = lax.rem(me + k, T)
        remote(
            heads_send.at[u], heads_recv.at[u], heads_ssem.at[0], heads_rsem.at[u], tp(sibling)
        ).wait_recv()
    new_keys = []
    new_values = []
    for h in range(T):
        for g in range(group):
            turned[h, pl.ds(g * pad, pad), :] = turn(
                heads_recv[h, :, g * HEAD : (g + 1) * HEAD]
            )
        new_values.append(heads_recv[h, :, columns : columns + HEAD].astype(F32))
        new_keys.append(turn(heads_recv[h, :, columns + HEAD :]))

    scale = HEAD ** (-0.5)
    per = STEPS * group
    count = pairs.shape[1]
    for j in range(here):
        queries = []
        scores = []
        fresh = [[] for _ in range(STEPS)]
        for h in range(T):
            query = jnp.concatenate(
                [
                    turned[h, pl.ds(s * here + j, group, stride=pad), :]
                    for s in range(STEPS)
                ],
                axis=0,
            )
            keys = pairs[j, :, h * HEAD : (h + 1) * HEAD]
            scores.append(
                lax.dot_general(
                    query.astype(BF16),
                    keys,
                    (((1,), (1,)), ((), ())),
                    preferred_element_type=F32,
                )
            )
            for s in range(STEPS):
                at = s * here + j
                fresh[s].append(
                    jnp.sum(query * new_keys[h][at : at + 1, :], axis=1, keepdims=True)
                )
        score = jnp.concatenate(scores, axis=0) * scale
        lanes = iota((T * per, count), 1)
        valid = (lanes < 2 * length_ref[j]) & (lax.rem(lanes, 2) == 0)
        score = jnp.where(valid, score, -1e30)
        top = jnp.max(score, axis=1, keepdims=True)
        row_step = lax.rem(iota((T * per, 1), 0), per) // group
        new_scores = []
        for s in range(STEPS):
            new = jnp.concatenate(fresh[s], axis=0) * scale
            new = jnp.where(row_step >= s, new, -1e30)
            new_scores.append(new)
            top = jnp.maximum(top, new)
        old_exp = jnp.exp(score - top)
        total = jnp.sum(old_exp, axis=1, keepdims=True)
        new_exp = [jnp.exp(new - top) for new in new_scores]
        for new in new_exp:
            total = total + new
        inverse = 1.0 / total
        shifted = pltpu.roll(old_exp * inverse, 1, 1).astype(BF16)
        new_weight = [(new * inverse).astype(BF16).astype(F32) for new in new_exp]
        for h in range(T):
            part = slice(h * per, (h + 1) * per)
            result = dot(shifted[part], pairs[j, :, h * HEAD : (h + 1) * HEAD])
            for s in range(STEPS):
                at = s * here + j
                result = result + new_weight[s][part] * new_values[h][at : at + 1, :]
            for s in range(STEPS):
                results[h, pl.ds(s * here + j, group, stride=pad), :] = result[
                    s * group : (s + 1) * group
                ]
    for h in range(T):
        for g in range(group):
            back_send[h, :, g * HEAD : (g + 1) * HEAD] = results[
                h, pl.ds(g * pad, pad), :
            ].astype(BF16)
    for k in range(1, T):
        u = lax.rem(me + k, T)
        send(
            remote(back_send.at[u], back_recv.at[me], back_ssem.at[k], back_rsem.at[me], tp(u))
        )
    back_recv[me] = back_send[me]
    collect = spread((rows, T * pad), 1, 0)
    for k in range(1, T):
        u = lax.rem(me + k, T)
        remote(
            back_send.at[u], back_recv.at[u], back_ssem.at[0], back_rsem.at[u], tp(sibling)
        ).wait_recv()
    attended = dot(collect, back_recv[...].reshape(T * pad, columns)).astype(BF16)

    parts = own_part.shape[1]
    piece = width // parts

    def multiply(i, p):
        lanes = pl.ds(p * piece, piece)
        u = targets[i] * CORES + (1 - core)
        v = targets[i] * CORES + core
        if p == 0:
            wide_copy(u).wait()
            wide_copy(v).wait()
        sib_send[i, p] = dot(attended, wide_out[u, :, lanes]).astype(BF16)
        send(
            remote(
                sib_send.at[i, p],
                sib_recv.at[i, p],
                sib_ssem.at[i, p],
                sib_rsem.at[i, p],
                tp(sibling),
            )
        )
        own_part[i, p] = dot(attended, wide_out[v, :, lanes])

    def take(i, v, p, way, condition):
        @pl.when(condition)
        def _():
            remote(
                sum_send.at[i, p],
                sum_recv.at[way, v, p],
                sum_ssem.at[i, p],
                sum_rsem.at[way, v, p],
                tp(sibling),
            ).wait_recv()
            own_part[i, p] += sum_recv[way, v, p].astype(F32)

    def finish(i, p):
        remote(
            sib_send.at[i, p], sib_recv.at[i, p], sib_ssem.at[i, p], sib_rsem.at[i, p], tp(sibling)
        ).wait_recv()
        own_part[i, p] += sib_recv[i, p].astype(F32)
        v = targets[i]
        if i == last:
            take(i, v, p, 0, z > 0)
            take(i, v, p, 1, z < last)
            return
        take(i, v, p, 0, (v > z) & (z > 0))
        take(i, v, p, 1, (v < z) & (z < last))
        sum_send[i, p] = own_part[i, p].astype(BF16)
        way = jnp.where(v > z, 0, 1)
        send(
            remote(
                sum_send.at[i, p],
                sum_recv.at[way, v, p],
                sum_ssem.at[i, p],
                sum_rsem.at[way, v, p],
                tp(me + jnp.where(v > z, CORES, -CORES)),
            )
        )

    items = [(i, p) for i in range(chips) for p in range(parts)]
    ahead = 2
    for item in items[:ahead]:
        multiply(*item)
    for n, item in enumerate(items):
        if n + ahead < len(items):
            multiply(*items[n + ahead])
        finish(*item)
    mixed = token + jnp.concatenate([own_part[last, p] for p in range(parts)], axis=1)
    for s in range(STEPS):
        out_ref[s] = mixed[s * requests : (s + 1) * requests].astype(BF16)
    for copy in sends:
        copy.wait_send()
    for condition, copy in maybe:
        pl.when(condition)(copy.wait_send)


def fused(
    tokens,
    input_norm_gain,
    query_weight,
    key_weight,
    value_weight,
    output_weight,
    adapter_down_maps,
    adapter_query_up,
    adapter_value_up,
    key_value_cache,
    cached_length,
    request_adapter_entry,
    group_adapter_ids,
    adapter_slot_table,
):
    T = lax.axis_size("tp")
    chips = T // CORES
    requests = tokens.shape[1]
    rows = STEPS * requests
    width = tokens.shape[2]
    here = cached_length.shape[0]
    owned = adapter_down_maps.shape[0]
    columns = query_weight.shape[1]
    group = columns // HEAD
    span = columns + HEAD
    pad = 16
    count = 2 * key_value_cache.shape[1]
    sizes = (T, requests, here, owned, group_adapter_ids.shape[1])
    whole = pl.BlockSpec(memory_space=pltpu.VMEM)
    scalar = pl.BlockSpec(memory_space=pltpu.SMEM)
    left = pl.BlockSpec(memory_space=pl.ANY)
    dma = pltpu.SemaphoreType.DMA
    vmem = pltpu.VMEM
    return pl.pallas_call(
        functools.partial(block_kernel, sizes),
        out_shape=jax.ShapeDtypeStruct(tokens.shape, BF16),
        in_specs=[whole] * 3 + [scalar] * 3 + [left] * 8,
        out_specs=whole,
        scratch_shapes=[
            vmem((T * width, span + HEAD), BF16),
            vmem((T, columns, width), BF16),
            vmem(adapter_down_maps.shape, BF16),
            vmem((owned, HEAD, span), BF16),
            vmem(key_value_cache.shape, BF16),
            vmem((here, count, KV_HEADS * HEAD), BF16),
            vmem((T, rows, width), BF16),
            vmem((2, rows, width), BF16),
            vmem((2, rows, HEAD), BF16),
            vmem((T, 16, HEAD), BF16),
            vmem((2, 8, HEAD), F32),
            vmem((rows, span + HEAD), F32),
            vmem((2, rows, HEAD), F32),
            vmem((rows, HEAD), F32),
            vmem((chips, rows, HEAD), F32),
            vmem((2, rows, HEAD), BF16),
            vmem((rows, span), F32),
            vmem((rows, span), BF16),
            vmem((rows, span), BF16),
            vmem((T, pad, span + HEAD), BF16),
            vmem((T, pad, span + HEAD), BF16),
            vmem((T, group * pad, HEAD), F32),
            vmem((T, group * pad, HEAD), F32),
            vmem((T, pad, columns), BF16),
            vmem((T, pad, columns), BF16),
            vmem((chips, 2, rows, width // 2), F32),
            vmem((chips, 2, rows, width // 2), BF16),
            vmem((chips, 2, rows, width // 2), BF16),
            vmem((chips, 2, rows, width // 2), BF16),
            vmem((2, chips, 2, rows, width // 2), BF16),
            dma((3, T)),
            dma((T,)),
            dma((1 + 2 * owned,)),
            dma(()),
            dma(()),
            dma((T,)),
            dma((chips, 2)),
            dma((chips,)),
            dma((3,)),
            dma((3,)),
            dma((T,)),
            dma((T,)),
            dma((2,)),
            dma((chips,)),
            dma((chips,)),
            dma((2,)),
            dma((2,)),
            dma((T,)),
            dma((T,)),
            dma((T,)),
            dma((T,)),
            dma((chips, 2)),
            dma((chips, 2)),
            dma((chips, 2)),
            dma((2, chips, 2)),
        ],
        compiler_params=pltpu.CompilerParams(
            collective_id=0, has_side_effects=True, vmem_limit_bytes=56 * 1024 * 1024
        ),
    )(
        tokens,
        input_norm_gain.reshape(1, width),
        request_adapter_entry.reshape(1, requests),
        group_adapter_ids,
        adapter_slot_table,
        cached_length,
        query_weight,
        key_weight,
        value_weight,
        output_weight,
        adapter_down_maps,
        adapter_query_up,
        adapter_value_up,
        key_value_cache,
    )


def device_program(*arrays):
    tokens, query_weight, key_weight, down = arrays[0], arrays[2], arrays[3], arrays[6]
    T = lax.axis_size("tp")
    whole_heads = (
        key_weight.shape[1] == HEAD
        and T == KV_HEADS
        and lax.axis_size("srv") == 2
        and down.shape[2] == HEAD
        and tokens.shape[2] == query_weight.shape[1]
        and tokens.shape[2] <= 13 * HEAD
        and (STEPS * tokens.shape[1]) % 16 == 0
        and STEPS * tokens.shape[1] <= HEAD
    )
    return fused(*arrays) if whole_heads else on_device(*arrays)


def solution(mesh):
    placed = (
        P(None, ("rep", "srv"), "tp"),
        P("tp"),
        P(None, "tp"),
        P(None, "tp"),
        P(None, "tp"),
        P("tp", None),
        P("srv", "tp", None),
        P("srv", None, "tp"),
        P("srv", None, "tp"),
        P(("rep", "srv", "tp"), None, None, None),
        P(("rep", "srv", "tp")),
        P(("rep", "srv")),
        P(),
        P(),
    )
    return jax.shard_map(
        device_program,
        mesh=mesh,
        in_specs=placed,
        out_specs=P(None, ("rep", "srv"), "tp"),
        check_vma=False,
    )
```

```python
import functools
import math

import jax
import jax.numpy as jnp
from jax import lax
from jax.experimental import pallas as pl
from jax.experimental.pallas import tpu as pltpu
from jax.sharding import PartitionSpec as P

KV_HEADS = 8
HEAD = 128
STEPS = 2
CORES = 2
MESH = pl.DeviceIdType.MESH
F32 = jnp.float32
BF16 = jnp.bfloat16


def normalize(values, gain):
    wide = values.astype(jnp.float32)
    scale = lax.rsqrt(jnp.mean(wide * wide, axis=-1, keepdims=True) + 1e-05)
    return (wide * scale * gain.astype(jnp.float32)).astype(jnp.bfloat16)


def rotate(block, position):
    half = block.shape[-1] // 2
    freq = jnp.exp(
        -(jnp.arange(half).astype(jnp.float32) * 2.0 / block.shape[-1]) * math.log(500000.0)
    )
    angle = position.astype(jnp.float32)[:, None, None] * freq
    cosine = jnp.cos(angle)
    sine = jnp.sin(angle)
    first = block[..., :half]
    second = block[..., half:]
    return jnp.concatenate(
        [first * cosine - second * sine, second * cosine + first * sine], axis=-1
    )


def attend(query, cache, length, new_keys, new_values):
    rows = query.shape[0]
    span = cache.shape[1]
    fresh = new_keys.shape[1]
    group = query.shape[1] // (KV_HEADS * HEAD)
    grouped = query.reshape(rows, KV_HEADS, group, HEAD)
    old_keys = cache[:, :, 0].reshape(rows, span, KV_HEADS, HEAD)
    old_values = cache[:, :, 1].reshape(rows, span, KV_HEADS, HEAD)
    keys_new = new_keys.reshape(rows, fresh, KV_HEADS, HEAD)
    values_new = new_values.reshape(rows, fresh, KV_HEADS, HEAD)
    factor = HEAD ** (-0.5)
    old_scores = (
        jnp.einsum("rkgd,rpkd->rkgp", grouped, old_keys, preferred_element_type=jnp.float32)
        * factor
    )
    valid = jnp.arange(span)[None, :] < length[:, None]
    old_scores = jnp.where(valid[:, None, None, :], old_scores, -jnp.inf)
    new_scores = (
        jnp.einsum("rkgd,rskd->rkgs", grouped, keys_new, preferred_element_type=jnp.float32)
        * factor
    )
    top = jnp.maximum(
        jnp.max(old_scores, axis=-1, keepdims=True), jnp.max(new_scores, axis=-1, keepdims=True)
    )
    old_exp = jnp.exp(old_scores - top)
    new_exp = jnp.exp(new_scores - top)
    total = jnp.sum(old_exp, axis=-1, keepdims=True) + jnp.sum(new_exp, axis=-1, keepdims=True)
    old_weight = (old_exp / total).astype(jnp.bfloat16)
    new_weight = (new_exp / total).astype(jnp.bfloat16)
    result = jnp.einsum(
        "rkgp,rpkd->rkgd", old_weight, old_values, preferred_element_type=jnp.float32
    )
    result = result + jnp.einsum(
        "rkgs,rskd->rkgd", new_weight, values_new, preferred_element_type=jnp.float32
    )
    return result.reshape(rows, KV_HEADS * group * HEAD).astype(jnp.bfloat16)


def on_device(
    tokens,
    input_norm_gain,
    query_weight,
    key_weight,
    value_weight,
    output_weight,
    adapter_down_maps,
    adapter_query_up,
    adapter_value_up,
    key_value_cache,
    cached_length,
    request_adapter_entry,
    group_adapter_ids,
    adapter_slot_table,
):
    group_index = lax.axis_index("srv")
    need = group_adapter_ids.shape[1]
    every = (
        lax.all_gather(adapter_down_maps, "srv", axis=0, tiled=True),
        lax.all_gather(adapter_query_up, "srv", axis=0, tiled=True),
        lax.all_gather(adapter_value_up, "srv", axis=0, tiled=True),
    )
    wanted = adapter_slot_table[group_adapter_ids[group_index]]
    down_need = jnp.take(every[0], wanted, axis=0)
    up_query_need = jnp.take(every[1], wanted, axis=0)
    up_value_need = jnp.take(every[2], wanted, axis=0)
    picks = (request_adapter_entry[:, None] == jnp.arange(need)[None, :]).astype(jnp.float32)
    rank = up_query_need.shape[1]

    def attend_step(step, query_rows, key_steps, value_steps):
        rows = query_rows.shape[0]
        turned = (
            rotate(query_rows.astype(jnp.float32).reshape(rows, -1, HEAD), cached_length + step)
            .astype(jnp.bfloat16)
            .reshape(rows, -1)
        )
        fresh_keys = jnp.stack(
            [
                rotate(key_steps[s].astype(jnp.float32).reshape(rows, -1, HEAD), cached_length + s)
                .astype(jnp.bfloat16)
                .reshape(rows, -1)
                for s in range(step + 1)
            ],
            axis=1,
        )
        fresh_values = jnp.stack([value_steps[s] for s in range(step + 1)], axis=1)
        return attend(turned, key_value_cache, cached_length, fresh_keys, fresh_values)

    steps_here = tokens.shape[0]
    width = tokens.shape[2]
    flat = tokens.reshape(-1, width)
    whole = lax.all_gather(flat, "tp", axis=1, tiled=True)
    gain = lax.all_gather(input_norm_gain, "tp", axis=0, tiled=True)
    normed_input = normalize(whole, gain)
    mine = lax.dynamic_slice_in_dim(normed_input, lax.axis_index("tp") * width, width, 1)
    row_picks = jnp.tile(picks, (steps_here, 1))[:, :, None]
    partial_value = jnp.einsum("md,ndk->mnk", mine, down_need, preferred_element_type=jnp.float32)
    shrunk = jnp.sum(partial_value * row_picks, axis=1)
    rank_row_values = lax.psum(shrunk, "tp").astype(jnp.bfloat16)
    query_lift = jnp.einsum(
        "mk,nkc->mnc", rank_row_values[:, :rank], up_query_need, preferred_element_type=jnp.float32
    )
    value_lift = jnp.einsum(
        "mk,nkc->mnc", rank_row_values[:, rank:], up_value_need, preferred_element_type=jnp.float32
    )
    query = (
        jnp.dot(normed_input, query_weight, preferred_element_type=jnp.float32)
        + jnp.sum(query_lift * row_picks, axis=1)
    ).astype(jnp.bfloat16)
    keys = jnp.dot(normed_input, key_weight, preferred_element_type=jnp.float32).astype(
        jnp.bfloat16
    )
    values = (
        jnp.dot(normed_input, value_weight, preferred_element_type=jnp.float32)
        + jnp.sum(value_lift * row_picks, axis=1)
    ).astype(jnp.bfloat16)

    def by_step(array):
        return array.reshape(steps_here, -1, array.shape[1])

    query, keys, values = (
        lax.all_to_all(by_step(query), "tp", split_axis=1, concat_axis=2, tiled=True),
        lax.all_to_all(by_step(keys), "tp", split_axis=1, concat_axis=2, tiled=True),
        lax.all_to_all(by_step(values), "tp", split_axis=1, concat_axis=2, tiled=True),
    )
    attended = [attend_step(step, query[step], keys, values) for step in range(STEPS)]
    finish_attended = jnp.stack(attended)
    heads = lax.all_to_all(finish_attended, "tp", split_axis=2, concat_axis=1, tiled=True)
    flat_heads = heads.reshape(-1, heads.shape[2])
    summed = lax.psum_scatter(
        lax.dot_general(
            output_weight, flat_heads, (((0,), (1,)), ((), ())), preferred_element_type=jnp.float32
        ),
        "tp",
        scatter_dimension=0,
        tiled=True,
    )
    return (tokens.astype(jnp.float32) + summed.T.reshape(tokens.shape)).astype(jnp.bfloat16)


def remote(src, dst, send, recv, device):
    return pltpu.make_async_remote_copy(
        src_ref=src,
        dst_ref=dst,
        send_sem=send,
        recv_sem=recv,
        device_id=device,
        device_id_type=MESH,
    )


def iota(shape, axis):
    return lax.broadcasted_iota(jnp.int32, shape, axis)


def dot(left, right):
    return jnp.dot(left, right, preferred_element_type=F32)


def block_kernel(
    sizes,
    tokens_ref,
    gain_ref,
    entry_ref,
    ids_ref,
    table_ref,
    length_ref,
    query_w,
    key_w,
    value_w,
    out_w,
    down_hbm,
    up_query_hbm,
    up_value_hbm,
    cache_hbm,
    out_ref,
    weight,
    wide_out,
    down,
    up,
    cache,
    pairs,
    gathered,
    raw,
    masks,
    stats,
    totals,
    acc,
    half_send,
    half_recv,
    chip_sum,
    ranks,
    lift_own,
    lift_send,
    lift_recv,
    heads_send,
    heads_recv,
    turned,
    results,
    back_send,
    back_recv,
    own_part,
    sib_send,
    sib_recv,
    sum_send,
    sum_recv,
    weight_sem,
    wide_sem,
    small_sem,
    cache_sem,
    x_send,
    x_recv,
    line_send,
    forward_send,
    peer_send,
    peer_recv,
    stat_send,
    stat_recv,
    half_sem,
    chip_send,
    chip_recv,
    rank_sem,
    lift_sem,
    heads_ssem,
    heads_rsem,
    back_ssem,
    back_rsem,
    sib_ssem,
    sib_rsem,
    sum_ssem,
    sum_rsem,
):
    T, requests, here, owned, need = sizes
    chips = T // CORES
    rows = STEPS * requests
    width = tokens_ref.shape[2]
    columns = query_w.shape[1]
    group = columns // HEAD
    pad = 16
    me = lax.axis_index("tp")
    side = lax.axis_index("srv")
    z = me // CORES
    core = lax.rem(me, CORES)
    sibling = z * CORES + (1 - core)
    other = 1 - side

    def tp(index):
        return {"tp": index}

    def at_chip(k):
        return lax.rem(z + k, chips)

    peer = {"srv": other}
    last = chips - 1

    def pick(lists, i):
        value = lists[0][i]
        for at in range(1, chips):
            value = jnp.where(z == at, lists[at][i], value)
        return value

    near = [
        sorted((v for v in range(chips) if v != at), key=lambda v: (abs(v - at), v))
        for at in range(chips)
    ]

    def ready(at, v):
        if v == at:
            return 4 * chips
        return at + last - v if v > at else last - at + v

    onward = [
        sorted(range(chips), key=lambda v: (ready(at, v), abs(v - at))) for at in range(chips)
    ]
    sources = [pick(near, i) for i in range(last)]
    targets = [pick(onward, i) for i in range(chips)]

    def weight_copies(u):
        span = pl.ds(pl.multiple_of(u * width, width), width)
        return (
            pltpu.make_async_copy(
                query_w.at[span, :], weight.at[span, pl.ds(0, columns)], weight_sem.at[0, u]
            ),
            pltpu.make_async_copy(
                value_w.at[span, :], weight.at[span, pl.ds(columns, HEAD)], weight_sem.at[1, u]
            ),
            pltpu.make_async_copy(
                key_w.at[span, :], weight.at[span, pl.ds(columns + HEAD, HEAD)], weight_sem.at[2, u]
            ),
        )

    def wide_copy(u):
        span = pl.ds(pl.multiple_of(u * width, width), width)
        return pltpu.make_async_copy(out_w.at[:, span], wide_out.at[u], wide_sem.at[u])

    small = [pltpu.make_async_copy(down_hbm, down, small_sem.at[0])]
    for a in range(owned):
        small.append(
            pltpu.make_async_copy(
                up_query_hbm.at[a],
                up.at[a, pl.ds(0, HEAD // 2), pl.ds(0, columns)],
                small_sem.at[1 + a],
            )
        )
        small.append(
            pltpu.make_async_copy(
                up_value_hbm.at[a],
                up.at[a, pl.ds(HEAD // 2, HEAD // 2), pl.ds(columns, HEAD)],
                small_sem.at[1 + owned + a],
            )
        )
    order = [me, sibling]
    for v in sources:
        order += [v * CORES + core, v * CORES + (1 - core)]
    for copy in weight_copies(me):
        copy.start()
    for copy in small:
        copy.start()
    cache_copy = pltpu.make_async_copy(cache_hbm, cache, cache_sem)
    wide_order = []
    for v in targets:
        wide_order += [v * CORES + (1 - core), v * CORES + core]

    early = 3
    begun = [1]

    def begin(upto):
        for u in order[begun[0] : upto]:
            for copy in weight_copies(u):
                copy.start()
        begun[0] = max(begun[0], upto)

    barrier = pltpu.get_barrier_semaphore()
    for k in range(1, T):
        pl.semaphore_signal(
            barrier, inc=1, device_id=tp(lax.rem(me + k, T)), device_id_type=MESH
        )
    pl.semaphore_signal(barrier, inc=1, device_id=peer, device_id_type=MESH)

    token = jnp.concatenate([tokens_ref[s].astype(F32) for s in range(STEPS)], axis=0)
    raw[side] = token.astype(BF16)
    square = jnp.sum(token * token, axis=1, keepdims=True)
    eye = iota((rows, HEAD), 0) == iota((rows, HEAD), 1)
    square = jnp.sum(jnp.where(eye, square, 0.0), axis=0, keepdims=True)
    high = square.astype(BF16).astype(F32)
    middle = (square - high).astype(BF16).astype(F32)
    low = square - high - middle
    gain = gain_ref[...].astype(F32)
    gain_rows = width // HEAD
    stats[me] = jnp.concatenate(
        [gain[:, i * HEAD : (i + 1) * HEAD] for i in range(gain_rows)]
        + [high, middle, low, jnp.zeros((16 - 3 - gain_rows, HEAD), F32)],
        axis=0,
    ).astype(BF16)
    request = lax.rem(iota((rows, requests), 0), requests)
    entry = jnp.sum(
        jnp.where(request == iota((rows, requests), 1), entry_ref[...], 0), axis=1, keepdims=True
    )
    slot = jnp.zeros((rows, 1), jnp.int32)
    for n in range(need):
        slot = jnp.where(entry == n, table_ref[ids_ref[side, n]], slot)
    masks[side] = jnp.where(slot == iota((rows, HEAD), 1), 1.0, 0.0).astype(BF16)

    pl.semaphore_wait(barrier, T)
    sends = []

    def send(copy):
        copy.start()
        sends.append(copy)

    mine = raw.at[side]
    send(remote(masks.at[side], masks.at[side], peer_send.at[1], peer_recv.at[1], peer))
    send(remote(mine, raw.at[side], peer_send.at[0], peer_recv.at[0], peer))
    for k in range(1, T):
        send(
            remote(
                stats.at[me], stats.at[me], stat_send.at[k], stat_recv.at[me], tp(lax.rem(me + k, T))
            )
        )

    def conditional(condition, copy):
        @pl.when(condition)
        def _():
            copy.start()

        maybe.append((condition, copy))

    maybe = []

    def along(u, block, right, left, i):
        for condition, step, s in ((right, 1, 0), (left, -1, 1)):
            conditional(
                condition,
                remote(
                    block, gathered.at[u], line_send.at[i, s], x_recv.at[u], tp(me + step * CORES)
                ),
            )

    along(me, mine, z < last, z > 0, 0)
    send(remote(mine, gathered.at[me], x_send, x_recv.at[me], tp(sibling)))
    begin(early)

    for a in range(owned):
        up[a, pl.ds(HEAD // 2, HEAD // 2), pl.ds(0, columns)] = jnp.zeros(
            (HEAD // 2, columns), BF16
        )
        up[a, pl.ds(0, HEAD // 2), pl.ds(columns, HEAD)] = jnp.zeros((HEAD // 2, HEAD), BF16)

    used = [0]

    def project(u, x):
        for copy in weight_copies(u):
            copy.wait()
        used[0] += 1
        begin(used[0] + early)
        return dot(x, weight[pl.ds(pl.multiple_of(u * width, width), width), :])


    for copy in small:
        copy.wait()

    def mask_of(side_rows, a):
        lane = iota((rows, HEAD), 1)
        picked = jnp.where(lane == side * owned + a, masks[side_rows].astype(F32), 0.0)
        return jnp.sum(picked, axis=1, keepdims=True)

    def shrink(side_rows):
        x = (raw[side_rows].astype(F32) * gain).astype(BF16)
        total = jnp.zeros((rows, HEAD), F32)
        for a in range(owned):
            total = total + dot(x, down[a]) * mask_of(side_rows, a)
        half_send[side_rows] = total

    shrink(side)

    def squares_of(u):
        block = stats[u].astype(F32)
        top_row = gain_rows
        return (
            block[top_row : top_row + 1]
            + block[top_row + 1 : top_row + 2]
            + block[top_row + 2 : top_row + 3]
        )

    def gain_of(u):
        block = stats[u].astype(F32)
        return jnp.concatenate([block[i : i + 1] for i in range(gain_rows)], axis=1)

    def factor_of(total):
        column = jnp.sum(
            jnp.where(eye, jnp.broadcast_to(total, (rows, HEAD)), 0.0), axis=1, keepdims=True
        )
        return lax.rsqrt(column / (T * width) + 1e-05)

    total_square = squares_of(me)
    for k in range(1, T):
        u = lax.rem(me + k, T)
        remote(
            stats.at[me], stats.at[u], stat_send.at[0], stat_recv.at[u], tp(sibling)
        ).wait_recv()
        total_square = total_square + squares_of(u)
    totals[side] = jnp.broadcast_to(total_square, (8, HEAD))
    send(remote(totals.at[side], totals.at[side], peer_send.at[2], peer_recv.at[2], peer))
    factor = factor_of(total_square)

    def normed(block, row_factor, u):
        return (block.astype(F32) * row_factor * gain_of(u)).astype(BF16)

    acc[...] = project(me, normed(raw[side], factor, me))

    def wait_x(u):
        remote(mine, gathered.at[u], x_send, x_recv.at[u], tp(sibling)).wait_recv()

    def add_block(u):
        acc[...] += project(u, normed(gathered[u], factor, u))

    def arrive(i):
        v = sources[i]
        u = v * CORES + core
        wait_x(u)
        along(u, gathered.at[u], (v < z) & (z < last), (v > z) & (z > 0), i + 1)
        send(
            remote(gathered.at[u], gathered.at[u], forward_send.at[i], x_recv.at[u], tp(sibling))
        )

    def add_same(i):
        add_block(sources[i] * CORES + core)

    def add_other(i):
        u = sources[i] * CORES + (1 - core)
        wait_x(u)
        add_block(u)

    arrive(0)
    remote(masks.at[side], masks.at[other], peer_send.at[1], peer_recv.at[1], peer).wait_recv()
    remote(mine, raw.at[other], peer_send.at[0], peer_recv.at[0], peer).wait_recv()
    shrink(other)
    half = remote(
        half_send.at[1 - core], half_recv, half_sem.at[0], half_sem.at[1], tp(sibling)
    )
    send(half)
    wait_x(sibling)
    add_block(sibling)
    half.wait_recv()
    chip_total = half_send[core] + half_recv[...]
    chip_sum[z] = chip_total.astype(chip_sum.dtype)
    for k in range(1, chips):
        send(
            remote(
                chip_sum.at[z],
                chip_sum.at[z],
                chip_send.at[k],
                chip_recv.at[z],
                tp(at_chip(k) * CORES + core),
            )
        )
    add_same(0)
    arrive(1)
    add_other(0)
    add_same(1)
    for k in range(1, chips):
        v = at_chip(k)
        remote(
            chip_sum.at[z], chip_sum.at[v], chip_send.at[0], chip_recv.at[v], tp(sibling)
        ).wait_recv()
        chip_total = chip_total + chip_sum[v].astype(F32)
    remote(totals.at[side], totals.at[other], peer_send.at[2], peer_recv.at[2], peer).wait_recv()
    ranks[core] = (chip_total * factor_of(totals[core][0:1])).astype(BF16)
    rank_copy = remote(
        ranks.at[core], ranks.at[core], rank_sem.at[0], rank_sem.at[1], tp(sibling)
    )
    send(rank_copy)
    add_other(1)
    remote(
        ranks.at[core], ranks.at[1 - core], rank_sem.at[0], rank_sem.at[1], tp(sibling)
    ).wait_recv()

    def lift(side_rows):
        rank = ranks[side_rows].astype(F32)
        total = jnp.zeros((rows, columns + HEAD), F32)
        for a in range(owned):
            total = total + dot((rank * mask_of(side_rows, a)).astype(BF16), up[a])
        return total

    lift_send[...] = lift(other).astype(BF16)
    lift_copy = remote(lift_send, lift_recv, lift_sem.at[0], lift_sem.at[1], peer)
    send(lift_copy)
    lift_own[...] = lift(side)
    for i in range(2, last):
        arrive(i)
        if i == last - 1:
            cache_copy.start()
        add_same(i)
        add_other(i)
    lift_copy.wait_recv()
    span = columns + HEAD
    front = (acc[:, 0:span] + lift_own[...] + lift_recv[...].astype(F32)).astype(BF16)
    key_block = acc[:, span:].astype(BF16)

    def spread(shape, row_axis, col_axis):
        row = iota(shape, row_axis)
        u = row // pad
        i = lax.rem(row, pad)
        step = i // here
        source = step * requests + u * here + lax.rem(i, here)
        return jnp.where(
            (i < STEPS * here) & (iota(shape, col_axis) == source), 1.0, 0.0
        ).astype(BF16)

    place = spread((T * pad, rows), 0, 1)
    heads_send[:, :, 0:span] = dot(place, front).astype(BF16).reshape(T, pad, span)
    heads_send[:, :, span:] = dot(place, key_block).astype(BF16).reshape(T, pad, HEAD)
    for k in range(1, T):
        u = lax.rem(me + k, T)
        send(
            remote(
                heads_send.at[u], heads_recv.at[me], heads_ssem.at[k], heads_rsem.at[me], tp(u)
            )
        )
    heads_recv[me] = heads_send[me]
    for u in wide_order:
        wide_copy(u).start()
    cache_copy.wait()
    for j in range(here):
        pairs[j] = cache[j].reshape(pairs.shape[1], pairs.shape[2])

    row = iota((pad, HEAD), 0)
    lane = iota((pad, HEAD), 1)
    step = row // here
    index = lax.rem(row, here)
    position = jnp.zeros((pad, HEAD), jnp.int32)
    for j in range(here):
        position = jnp.where(index == j, length_ref[j], position)
    position = (position + step).astype(F32)
    freq = jnp.exp(
        -(lax.rem(lane, HEAD // 2).astype(F32) * 2.0 / HEAD) * math.log(500000.0)
    )
    angle = position * freq
    cosine = jnp.cos(angle)
    sine = jnp.where(lane < HEAD // 2, -jnp.sin(angle), jnp.sin(angle))

    def turn(block):
        wide = block.astype(F32)
        return (wide * cosine + pltpu.roll(wide, HEAD // 2, 1) * sine).astype(BF16).astype(F32)

    results[...] = jnp.zeros(results.shape, F32)
    for k in range(1, T):
        u = lax.rem(me + k, T)
        remote(
            heads_send.at[u], heads_recv.at[u], heads_ssem.at[0], heads_rsem.at[u], tp(sibling)
        ).wait_recv()
    new_keys = []
    new_values = []
    for h in range(T):
        for g in range(group):
            turned[h, pl.ds(g * pad, pad), :] = turn(
                heads_recv[h, :, g * HEAD : (g + 1) * HEAD]
            )
        new_values.append(heads_recv[h, :, columns : columns + HEAD].astype(F32))
        new_keys.append(turn(heads_recv[h, :, columns + HEAD :]))

    scale = HEAD ** (-0.5)
    per = STEPS * group
    count = pairs.shape[1]
    for j in range(here):
        queries = []
        scores = []
        fresh = [[] for _ in range(STEPS)]
        for h in range(T):
            query = jnp.concatenate(
                [
                    turned[h, pl.ds(s * here + j, group, stride=pad), :]
                    for s in range(STEPS)
                ],
                axis=0,
            )
            keys = pairs[j, :, h * HEAD : (h + 1) * HEAD]
            scores.append(
                lax.dot_general(
                    query.astype(BF16),
                    keys,
                    (((1,), (1,)), ((), ())),
                    preferred_element_type=F32,
                )
            )
            for s in range(STEPS):
                at = s * here + j
                fresh[s].append(
                    jnp.sum(query * new_keys[h][at : at + 1, :], axis=1, keepdims=True)
                )
        score = jnp.concatenate(scores, axis=0) * scale
        lanes = iota((T * per, count), 1)
        valid = (lanes < 2 * length_ref[j]) & (lax.rem(lanes, 2) == 0)
        score = jnp.where(valid, score, -1e30)
        top = jnp.max(score, axis=1, keepdims=True)
        row_step = lax.rem(iota((T * per, 1), 0), per) // group
        new_scores = []
        for s in range(STEPS):
            new = jnp.concatenate(fresh[s], axis=0) * scale
            new = jnp.where(row_step >= s, new, -1e30)
            new_scores.append(new)
            top = jnp.maximum(top, new)
        old_exp = jnp.exp(score - top)
        total = jnp.sum(old_exp, axis=1, keepdims=True)
        new_exp = [jnp.exp(new - top) for new in new_scores]
        for new in new_exp:
            total = total + new
        inverse = 1.0 / total
        shifted = pltpu.roll(old_exp * inverse, 1, 1).astype(BF16)
        new_weight = [(new * inverse).astype(BF16).astype(F32) for new in new_exp]
        for h in range(T):
            part = slice(h * per, (h + 1) * per)
            result = dot(shifted[part], pairs[j, :, h * HEAD : (h + 1) * HEAD])
            for s in range(STEPS):
                at = s * here + j
                result = result + new_weight[s][part] * new_values[h][at : at + 1, :]
            for s in range(STEPS):
                results[h, pl.ds(s * here + j, group, stride=pad), :] = result[
                    s * group : (s + 1) * group
                ]
    for h in range(T):
        for g in range(group):
            back_send[h, :, g * HEAD : (g + 1) * HEAD] = results[
                h, pl.ds(g * pad, pad), :
            ].astype(BF16)
    for k in range(1, T):
        u = lax.rem(me + k, T)
        send(
            remote(back_send.at[u], back_recv.at[me], back_ssem.at[k], back_rsem.at[me], tp(u))
        )
    back_recv[me] = back_send[me]
    collect = spread((rows, T * pad), 1, 0)
    for k in range(1, T):
        u = lax.rem(me + k, T)
        remote(
            back_send.at[u], back_recv.at[u], back_ssem.at[0], back_rsem.at[u], tp(sibling)
        ).wait_recv()
    attended = dot(collect, back_recv[...].reshape(T * pad, columns)).astype(BF16)

    parts = own_part.shape[1]
    piece = width // parts

    def multiply(i, p):
        lanes = pl.ds(p * piece, piece)
        u = targets[i] * CORES + (1 - core)
        v = targets[i] * CORES + core
        if p == 0:
            wide_copy(u).wait()
            wide_copy(v).wait()
        sib_send[i, p] = dot(attended, wide_out[u, :, lanes]).astype(BF16)
        send(
            remote(
                sib_send.at[i, p],
                sib_recv.at[i, p],
                sib_ssem.at[i, p],
                sib_rsem.at[i, p],
                tp(sibling),
            )
        )
        own_part[i, p] = dot(attended, wide_out[v, :, lanes])

    def take(i, v, p, way, condition):
        @pl.when(condition)
        def _():
            remote(
                sum_send.at[i, p],
                sum_recv.at[way, v, p],
                sum_ssem.at[i, p],
                sum_rsem.at[way, v, p],
                tp(sibling),
            ).wait_recv()
            own_part[i, p] += sum_recv[way, v, p].astype(F32)

    def finish(i, p):
        remote(
            sib_send.at[i, p], sib_recv.at[i, p], sib_ssem.at[i, p], sib_rsem.at[i, p], tp(sibling)
        ).wait_recv()
        own_part[i, p] += sib_recv[i, p].astype(F32)
        v = targets[i]
        if i == last:
            take(i, v, p, 0, z > 0)
            take(i, v, p, 1, z < last)
            return
        take(i, v, p, 0, (v > z) & (z > 0))
        take(i, v, p, 1, (v < z) & (z < last))
        sum_send[i, p] = own_part[i, p].astype(BF16)
        way = jnp.where(v > z, 0, 1)
        send(
            remote(
                sum_send.at[i, p],
                sum_recv.at[way, v, p],
                sum_ssem.at[i, p],
                sum_rsem.at[way, v, p],
                tp(me + jnp.where(v > z, CORES, -CORES)),
            )
        )

    items = [(i, p) for i in range(chips) for p in range(parts)]
    ahead = 1
    for item in items[:ahead]:
        multiply(*item)
    for n, item in enumerate(items):
        if n + ahead < len(items):
            multiply(*items[n + ahead])
        finish(*item)
    mixed = token + jnp.concatenate([own_part[last, p] for p in range(parts)], axis=1)
    for s in range(STEPS):
        out_ref[s] = mixed[s * requests : (s + 1) * requests].astype(BF16)
    for copy in sends:
        copy.wait_send()
    for condition, copy in maybe:
        pl.when(condition)(copy.wait_send)


def fused(
    tokens,
    input_norm_gain,
    query_weight,
    key_weight,
    value_weight,
    output_weight,
    adapter_down_maps,
    adapter_query_up,
    adapter_value_up,
    key_value_cache,
    cached_length,
    request_adapter_entry,
    group_adapter_ids,
    adapter_slot_table,
):
    T = lax.axis_size("tp")
    chips = T // CORES
    requests = tokens.shape[1]
    rows = STEPS * requests
    width = tokens.shape[2]
    here = cached_length.shape[0]
    owned = adapter_down_maps.shape[0]
    columns = query_weight.shape[1]
    group = columns // HEAD
    span = columns + HEAD
    pad = 16
    count = 2 * key_value_cache.shape[1]
    sizes = (T, requests, here, owned, group_adapter_ids.shape[1])
    whole = pl.BlockSpec(memory_space=pltpu.VMEM)
    scalar = pl.BlockSpec(memory_space=pltpu.SMEM)
    left = pl.BlockSpec(memory_space=pl.ANY)
    dma = pltpu.SemaphoreType.DMA
    vmem = pltpu.VMEM
    return pl.pallas_call(
        functools.partial(block_kernel, sizes),
        out_shape=jax.ShapeDtypeStruct(tokens.shape, BF16),
        in_specs=[whole] * 3 + [scalar] * 3 + [left] * 8,
        out_specs=whole,
        scratch_shapes=[
            vmem((T * width, span + HEAD), BF16),
            vmem((T, columns, width), BF16),
            vmem(adapter_down_maps.shape, BF16),
            vmem((owned, HEAD, span), BF16),
            vmem(key_value_cache.shape, BF16),
            vmem((here, count, KV_HEADS * HEAD), BF16),
            vmem((T, rows, width), BF16),
            vmem((2, rows, width), BF16),
            vmem((2, rows, HEAD), BF16),
            vmem((T, 16, HEAD), BF16),
            vmem((2, 8, HEAD), F32),
            vmem((rows, span + HEAD), F32),
            vmem((2, rows, HEAD), F32),
            vmem((rows, HEAD), F32),
            vmem((chips, rows, HEAD), F32),
            vmem((2, rows, HEAD), BF16),
            vmem((rows, span), F32),
            vmem((rows, span), BF16),
            vmem((rows, span), BF16),
            vmem((T, pad, span + HEAD), BF16),
            vmem((T, pad, span + HEAD), BF16),
            vmem((T, group * pad, HEAD), F32),
            vmem((T, group * pad, HEAD), F32),
            vmem((T, pad, columns), BF16),
            vmem((T, pad, columns), BF16),
            vmem((chips, 2, rows, width // 2), F32),
            vmem((chips, 2, rows, width // 2), BF16),
            vmem((chips, 2, rows, width // 2), BF16),
            vmem((chips, 2, rows, width // 2), BF16),
            vmem((2, chips, 2, rows, width // 2), BF16),
            dma((3, T)),
            dma((T,)),
            dma((1 + 2 * owned,)),
            dma(()),
            dma(()),
            dma((T,)),
            dma((chips, 2)),
            dma((chips,)),
            dma((3,)),
            dma((3,)),
            dma((T,)),
            dma((T,)),
            dma((2,)),
            dma((chips,)),
            dma((chips,)),
            dma((2,)),
            dma((2,)),
            dma((T,)),
            dma((T,)),
            dma((T,)),
            dma((T,)),
            dma((chips, 2)),
            dma((chips, 2)),
            dma((chips, 2)),
            dma((2, chips, 2)),
        ],
        compiler_params=pltpu.CompilerParams(
            collective_id=0, has_side_effects=True, vmem_limit_bytes=56 * 1024 * 1024
        ),
    )(
        tokens,
        input_norm_gain.reshape(1, width),
        request_adapter_entry.reshape(1, requests),
        group_adapter_ids,
        adapter_slot_table,
        cached_length,
        query_weight,
        key_weight,
        value_weight,
        output_weight,
        adapter_down_maps,
        adapter_query_up,
        adapter_value_up,
        key_value_cache,
    )


def device_program(*arrays):
    tokens, query_weight, key_weight, down = arrays[0], arrays[2], arrays[3], arrays[6]
    T = lax.axis_size("tp")
    whole_heads = (
        key_weight.shape[1] == HEAD
        and T == KV_HEADS
        and lax.axis_size("srv") == 2
        and down.shape[2] == HEAD
        and tokens.shape[2] == query_weight.shape[1]
        and tokens.shape[2] <= 13 * HEAD
        and (STEPS * tokens.shape[1]) % 16 == 0
        and STEPS * tokens.shape[1] <= HEAD
    )
    return fused(*arrays) if whole_heads else on_device(*arrays)


def solution(mesh):
    placed = (
        P(None, ("rep", "srv"), "tp"),
        P("tp"),
        P(None, "tp"),
        P(None, "tp"),
        P(None, "tp"),
        P("tp", None),
        P("srv", "tp", None),
        P("srv", None, "tp"),
        P("srv", None, "tp"),
        P(("rep", "srv", "tp"), None, None, None),
        P(("rep", "srv", "tp")),
        P(("rep", "srv")),
        P(),
        P(),
    )
    return jax.shard_map(
        device_program,
        mesh=mesh,
        in_specs=placed,
        out_specs=P(None, ("rep", "srv"), "tp"),
        check_vma=False,
    )
```

```python
import functools
import math

import jax
import jax.numpy as jnp
from jax import lax
from jax.experimental import pallas as pl
from jax.experimental.pallas import tpu as pltpu
from jax.sharding import PartitionSpec as P

KV_HEADS = 8
HEAD = 128
STEPS = 2
CORES = 2
MESH = pl.DeviceIdType.MESH
F32 = jnp.float32
BF16 = jnp.bfloat16


def normalize(values, gain):
    wide = values.astype(jnp.float32)
    scale = lax.rsqrt(jnp.mean(wide * wide, axis=-1, keepdims=True) + 1e-05)
    return (wide * scale * gain.astype(jnp.float32)).astype(jnp.bfloat16)


def rotate(block, position):
    half = block.shape[-1] // 2
    freq = jnp.exp(
        -(jnp.arange(half).astype(jnp.float32) * 2.0 / block.shape[-1]) * math.log(500000.0)
    )
    angle = position.astype(jnp.float32)[:, None, None] * freq
    cosine = jnp.cos(angle)
    sine = jnp.sin(angle)
    first = block[..., :half]
    second = block[..., half:]
    return jnp.concatenate(
        [first * cosine - second * sine, second * cosine + first * sine], axis=-1
    )


def attend(query, cache, length, new_keys, new_values):
    rows = query.shape[0]
    span = cache.shape[1]
    fresh = new_keys.shape[1]
    group = query.shape[1] // (KV_HEADS * HEAD)
    grouped = query.reshape(rows, KV_HEADS, group, HEAD)
    old_keys = cache[:, :, 0].reshape(rows, span, KV_HEADS, HEAD)
    old_values = cache[:, :, 1].reshape(rows, span, KV_HEADS, HEAD)
    keys_new = new_keys.reshape(rows, fresh, KV_HEADS, HEAD)
    values_new = new_values.reshape(rows, fresh, KV_HEADS, HEAD)
    factor = HEAD ** (-0.5)
    old_scores = (
        jnp.einsum("rkgd,rpkd->rkgp", grouped, old_keys, preferred_element_type=jnp.float32)
        * factor
    )
    valid = jnp.arange(span)[None, :] < length[:, None]
    old_scores = jnp.where(valid[:, None, None, :], old_scores, -jnp.inf)
    new_scores = (
        jnp.einsum("rkgd,rskd->rkgs", grouped, keys_new, preferred_element_type=jnp.float32)
        * factor
    )
    top = jnp.maximum(
        jnp.max(old_scores, axis=-1, keepdims=True), jnp.max(new_scores, axis=-1, keepdims=True)
    )
    old_exp = jnp.exp(old_scores - top)
    new_exp = jnp.exp(new_scores - top)
    total = jnp.sum(old_exp, axis=-1, keepdims=True) + jnp.sum(new_exp, axis=-1, keepdims=True)
    old_weight = (old_exp / total).astype(jnp.bfloat16)
    new_weight = (new_exp / total).astype(jnp.bfloat16)
    result = jnp.einsum(
        "rkgp,rpkd->rkgd", old_weight, old_values, preferred_element_type=jnp.float32
    )
    result = result + jnp.einsum(
        "rkgs,rskd->rkgd", new_weight, values_new, preferred_element_type=jnp.float32
    )
    return result.reshape(rows, KV_HEADS * group * HEAD).astype(jnp.bfloat16)


def on_device(
    tokens,
    input_norm_gain,
    query_weight,
    key_weight,
    value_weight,
    output_weight,
    adapter_down_maps,
    adapter_query_up,
    adapter_value_up,
    key_value_cache,
    cached_length,
    request_adapter_entry,
    group_adapter_ids,
    adapter_slot_table,
):
    group_index = lax.axis_index("srv")
    need = group_adapter_ids.shape[1]
    every = (
        lax.all_gather(adapter_down_maps, "srv", axis=0, tiled=True),
        lax.all_gather(adapter_query_up, "srv", axis=0, tiled=True),
        lax.all_gather(adapter_value_up, "srv", axis=0, tiled=True),
    )
    wanted = adapter_slot_table[group_adapter_ids[group_index]]
    down_need = jnp.take(every[0], wanted, axis=0)
    up_query_need = jnp.take(every[1], wanted, axis=0)
    up_value_need = jnp.take(every[2], wanted, axis=0)
    picks = (request_adapter_entry[:, None] == jnp.arange(need)[None, :]).astype(jnp.float32)
    rank = up_query_need.shape[1]

    def attend_step(step, query_rows, key_steps, value_steps):
        rows = query_rows.shape[0]
        turned = (
            rotate(query_rows.astype(jnp.float32).reshape(rows, -1, HEAD), cached_length + step)
            .astype(jnp.bfloat16)
            .reshape(rows, -1)
        )
        fresh_keys = jnp.stack(
            [
                rotate(key_steps[s].astype(jnp.float32).reshape(rows, -1, HEAD), cached_length + s)
                .astype(jnp.bfloat16)
                .reshape(rows, -1)
                for s in range(step + 1)
            ],
            axis=1,
        )
        fresh_values = jnp.stack([value_steps[s] for s in range(step + 1)], axis=1)
        return attend(turned, key_value_cache, cached_length, fresh_keys, fresh_values)

    steps_here = tokens.shape[0]
    width = tokens.shape[2]
    flat = tokens.reshape(-1, width)
    whole = lax.all_gather(flat, "tp", axis=1, tiled=True)
    gain = lax.all_gather(input_norm_gain, "tp", axis=0, tiled=True)
    normed_input = normalize(whole, gain)
    mine = lax.dynamic_slice_in_dim(normed_input, lax.axis_index("tp") * width, width, 1)
    row_picks = jnp.tile(picks, (steps_here, 1))[:, :, None]
    partial_value = jnp.einsum("md,ndk->mnk", mine, down_need, preferred_element_type=jnp.float32)
    shrunk = jnp.sum(partial_value * row_picks, axis=1)
    rank_row_values = lax.psum(shrunk, "tp").astype(jnp.bfloat16)
    query_lift = jnp.einsum(
        "mk,nkc->mnc", rank_row_values[:, :rank], up_query_need, preferred_element_type=jnp.float32
    )
    value_lift = jnp.einsum(
        "mk,nkc->mnc", rank_row_values[:, rank:], up_value_need, preferred_element_type=jnp.float32
    )
    query = (
        jnp.dot(normed_input, query_weight, preferred_element_type=jnp.float32)
        + jnp.sum(query_lift * row_picks, axis=1)
    ).astype(jnp.bfloat16)
    keys = jnp.dot(normed_input, key_weight, preferred_element_type=jnp.float32).astype(
        jnp.bfloat16
    )
    values = (
        jnp.dot(normed_input, value_weight, preferred_element_type=jnp.float32)
        + jnp.sum(value_lift * row_picks, axis=1)
    ).astype(jnp.bfloat16)

    def by_step(array):
        return array.reshape(steps_here, -1, array.shape[1])

    query, keys, values = (
        lax.all_to_all(by_step(query), "tp", split_axis=1, concat_axis=2, tiled=True),
        lax.all_to_all(by_step(keys), "tp", split_axis=1, concat_axis=2, tiled=True),
        lax.all_to_all(by_step(values), "tp", split_axis=1, concat_axis=2, tiled=True),
    )
    attended = [attend_step(step, query[step], keys, values) for step in range(STEPS)]
    finish_attended = jnp.stack(attended)
    heads = lax.all_to_all(finish_attended, "tp", split_axis=2, concat_axis=1, tiled=True)
    flat_heads = heads.reshape(-1, heads.shape[2])
    summed = lax.psum_scatter(
        lax.dot_general(
            output_weight, flat_heads, (((0,), (1,)), ((), ())), preferred_element_type=jnp.float32
        ),
        "tp",
        scatter_dimension=0,
        tiled=True,
    )
    return (tokens.astype(jnp.float32) + summed.T.reshape(tokens.shape)).astype(jnp.bfloat16)


def remote(src, dst, send, recv, device):
    return pltpu.make_async_remote_copy(
        src_ref=src,
        dst_ref=dst,
        send_sem=send,
        recv_sem=recv,
        device_id=device,
        device_id_type=MESH,
    )


def iota(shape, axis):
    return lax.broadcasted_iota(jnp.int32, shape, axis)


def dot(left, right):
    return jnp.dot(left, right, preferred_element_type=F32)


def block_kernel(
    sizes,
    tokens_ref,
    gain_ref,
    entry_ref,
    ids_ref,
    table_ref,
    length_ref,
    query_w,
    key_w,
    value_w,
    out_w,
    down_hbm,
    up_query_hbm,
    up_value_hbm,
    cache_hbm,
    out_ref,
    weight,
    wide_out,
    down,
    up,
    cache,
    pairs,
    gathered,
    raw,
    masks,
    stats,
    totals,
    acc,
    half_send,
    half_recv,
    chip_sum,
    ranks,
    lift_own,
    lift_send,
    lift_recv,
    heads_send,
    heads_recv,
    turned,
    results,
    back_send,
    back_recv,
    own_part,
    sib_send,
    sib_recv,
    sum_send,
    sum_recv,
    weight_sem,
    wide_sem,
    small_sem,
    cache_sem,
    x_send,
    x_recv,
    line_send,
    forward_send,
    peer_send,
    peer_recv,
    stat_send,
    stat_recv,
    half_sem,
    chip_send,
    chip_recv,
    rank_sem,
    lift_sem,
    heads_ssem,
    heads_rsem,
    back_ssem,
    back_rsem,
    sib_ssem,
    sib_rsem,
    sum_ssem,
    sum_rsem,
):
    T, requests, here, owned, need = sizes
    chips = T // CORES
    rows = STEPS * requests
    width = tokens_ref.shape[2]
    columns = query_w.shape[1]
    group = columns // HEAD
    pad = 16
    me = lax.axis_index("tp")
    side = lax.axis_index("srv")
    z = me // CORES
    core = lax.rem(me, CORES)
    sibling = z * CORES + (1 - core)
    other = 1 - side

    def tp(index):
        return {"tp": index}

    def at_chip(k):
        return lax.rem(z + k, chips)

    peer = {"srv": other}
    last = chips - 1

    def pick(lists, i):
        value = lists[0][i]
        for at in range(1, chips):
            value = jnp.where(z == at, lists[at][i], value)
        return value

    near = [
        sorted((v for v in range(chips) if v != at), key=lambda v: (abs(v - at), v))
        for at in range(chips)
    ]

    def ready(at, v):
        if v == at:
            return 4 * chips
        return at + last - v if v > at else last - at + v

    onward = [
        sorted(range(chips), key=lambda v: (ready(at, v), abs(v - at))) for at in range(chips)
    ]
    sources = [pick(near, i) for i in range(last)]
    targets = [pick(onward, i) for i in range(chips)]

    def weight_copies(u):
        span = pl.ds(pl.multiple_of(u * width, width), width)
        return (
            pltpu.make_async_copy(
                query_w.at[span, :], weight.at[span, pl.ds(0, columns)], weight_sem.at[0, u]
            ),
            pltpu.make_async_copy(
                value_w.at[span, :], weight.at[span, pl.ds(columns, HEAD)], weight_sem.at[1, u]
            ),
            pltpu.make_async_copy(
                key_w.at[span, :], weight.at[span, pl.ds(columns + HEAD, HEAD)], weight_sem.at[2, u]
            ),
        )

    def wide_copy(u):
        span = pl.ds(pl.multiple_of(u * width, width), width)
        return pltpu.make_async_copy(out_w.at[:, span], wide_out.at[u], wide_sem.at[u])

    small = []
    for a in range(owned):
        small.append(
            pltpu.make_async_copy(
                down_hbm.at[a], down.at[:, pl.ds(a * HEAD, HEAD)], small_sem.at[0, a]
            )
        )
        small.append(
            pltpu.make_async_copy(
                up_query_hbm.at[a],
                up.at[pl.ds(a * HEAD, HEAD // 2), pl.ds(0, columns)],
                small_sem.at[1, a],
            )
        )
        small.append(
            pltpu.make_async_copy(
                up_value_hbm.at[a],
                up.at[pl.ds(a * HEAD + HEAD // 2, HEAD // 2), pl.ds(columns, HEAD)],
                small_sem.at[2, a],
            )
        )
    order = [me, sibling]
    for v in sources:
        order += [v * CORES + core, v * CORES + (1 - core)]
    for copy in weight_copies(me):
        copy.start()
    for copy in small:
        copy.start()
    cache_copy = pltpu.make_async_copy(cache_hbm, cache, cache_sem)
    wide_order = []
    for v in targets:
        wide_order += [v * CORES + (1 - core), v * CORES + core]

    early = 3
    begun = [1]

    def begin(upto):
        for u in order[begun[0] : upto]:
            for copy in weight_copies(u):
                copy.start()
        begun[0] = max(begun[0], upto)

    barrier = pltpu.get_barrier_semaphore()
    for k in range(1, T):
        pl.semaphore_signal(
            barrier, inc=1, device_id=tp(lax.rem(me + k, T)), device_id_type=MESH
        )
    pl.semaphore_signal(barrier, inc=1, device_id=peer, device_id_type=MESH)

    token = jnp.concatenate([tokens_ref[s].astype(F32) for s in range(STEPS)], axis=0)
    raw[side] = token.astype(BF16)
    square = jnp.sum(token * token, axis=1, keepdims=True)
    eye = iota((rows, HEAD), 0) == iota((rows, HEAD), 1)
    square = jnp.sum(jnp.where(eye, square, 0.0), axis=0, keepdims=True)
    high = square.astype(BF16).astype(F32)
    middle = (square - high).astype(BF16).astype(F32)
    low = square - high - middle
    gain = gain_ref[...].astype(F32).reshape(1, width)
    gain_rows = width // HEAD
    stats[me] = jnp.concatenate(
        [gain[:, i * HEAD : (i + 1) * HEAD] for i in range(gain_rows)]
        + [high, middle, low, jnp.zeros((16 - 3 - gain_rows, HEAD), F32)],
        axis=0,
    ).astype(BF16)
    request = lax.rem(iota((rows, requests), 0), requests)
    entry = jnp.sum(
        jnp.where(request == iota((rows, requests), 1), entry_ref[...], 0), axis=1, keepdims=True
    )
    slot = jnp.zeros((rows, 1), jnp.int32)
    for n in range(need):
        slot = jnp.where(entry == n, table_ref[ids_ref[side, n]], slot)
    masks[side] = jnp.where(slot == iota((rows, HEAD), 1), 1.0, 0.0).astype(BF16)

    pl.semaphore_wait(barrier, T)
    sends = []

    def send(copy):
        copy.start()
        sends.append(copy)

    mine = raw.at[side]
    send(remote(masks.at[side], masks.at[side], peer_send.at[1], peer_recv.at[1], peer))
    send(remote(mine, raw.at[side], peer_send.at[0], peer_recv.at[0], peer))
    for k in range(1, T):
        send(
            remote(
                stats.at[me], stats.at[me], stat_send.at[k], stat_recv.at[me], tp(lax.rem(me + k, T))
            )
        )

    def conditional(condition, copy):
        @pl.when(condition)
        def _():
            copy.start()

        maybe.append((condition, copy))

    maybe = []

    def along(u, block, right, left, i):
        for condition, step, s in ((right, 1, 0), (left, -1, 1)):
            conditional(
                condition,
                remote(
                    block, gathered.at[u], line_send.at[i, s], x_recv.at[u], tp(me + step * CORES)
                ),
            )

    along(me, mine, z < last, z > 0, 0)
    send(remote(mine, gathered.at[me], x_send, x_recv.at[me], tp(sibling)))
    begin(early)

    for a in range(owned):
        up[pl.ds(a * HEAD + HEAD // 2, HEAD // 2), pl.ds(0, columns)] = jnp.zeros(
            (HEAD // 2, columns), BF16
        )
        up[pl.ds(a * HEAD, HEAD // 2), pl.ds(columns, HEAD)] = jnp.zeros((HEAD // 2, HEAD), BF16)

    used = [0]

    def project(u, x):
        for copy in weight_copies(u):
            copy.wait()
        used[0] += 1
        begin(used[0] + early)
        return dot(x, weight[pl.ds(pl.multiple_of(u * width, width), width), :])


    for copy in small:
        copy.wait()

    def mask_of(side_rows, a):
        lane = iota((rows, HEAD), 1)
        picked = jnp.where(lane == side * owned + a, masks[side_rows].astype(F32), 0.0)
        return jnp.sum(picked, axis=1, keepdims=True)

    def shrink(side_rows, x):
        every = dot(x, down[...])
        total = jnp.zeros((rows, HEAD), F32)
        for a in range(owned):
            total = total + every[:, a * HEAD : (a + 1) * HEAD] * mask_of(side_rows, a)
        half_send[side_rows] = total

    def squares_of(u):
        block = stats[u].astype(F32)
        top_row = gain_rows
        return (
            block[top_row : top_row + 1]
            + block[top_row + 1 : top_row + 2]
            + block[top_row + 2 : top_row + 3]
        )

    def gain_of(u):
        block = stats[u].astype(F32)
        return jnp.concatenate([block[i : i + 1] for i in range(gain_rows)], axis=1)

    def factor_of(total):
        column = jnp.sum(
            jnp.where(eye, jnp.broadcast_to(total, (rows, HEAD)), 0.0), axis=1, keepdims=True
        )
        return lax.rsqrt(column / (T * width) + 1e-05)

    total_square = squares_of(me)
    for k in range(1, T):
        u = lax.rem(me + k, T)
        remote(
            stats.at[me], stats.at[u], stat_send.at[0], stat_recv.at[u], tp(sibling)
        ).wait_recv()
        total_square = total_square + squares_of(u)
    totals[side] = jnp.broadcast_to(total_square, (8, HEAD))
    send(remote(totals.at[side], totals.at[side], peer_send.at[2], peer_recv.at[2], peer))
    factor = factor_of(total_square)

    def normed(block, row_factor, u):
        return (block.astype(F32) * row_factor * gain_of(u)).astype(BF16)

    normed_mine = normed(raw[side], factor, me)
    shrink(side, normed_mine)
    acc[...] = project(me, normed_mine)

    def wait_x(u):
        remote(mine, gathered.at[u], x_send, x_recv.at[u], tp(sibling)).wait_recv()

    def add_block(u):
        acc[...] += project(u, normed(gathered[u], factor, u))

    def arrive(i):
        v = sources[i]
        u = v * CORES + core
        wait_x(u)
        along(u, gathered.at[u], (v < z) & (z < last), (v > z) & (z > 0), i + 1)
        send(
            remote(gathered.at[u], gathered.at[u], forward_send.at[i], x_recv.at[u], tp(sibling))
        )

    def add_same(i):
        add_block(sources[i] * CORES + core)

    def add_other(i):
        u = sources[i] * CORES + (1 - core)
        wait_x(u)
        add_block(u)

    arrive(0)
    remote(masks.at[side], masks.at[other], peer_send.at[1], peer_recv.at[1], peer).wait_recv()
    remote(mine, raw.at[other], peer_send.at[0], peer_recv.at[0], peer).wait_recv()
    remote(totals.at[side], totals.at[other], peer_send.at[2], peer_recv.at[2], peer).wait_recv()
    shrink(other, normed(raw[other], factor_of(totals[other][0:1]), me))
    half = remote(
        half_send.at[1 - core], half_recv, half_sem.at[0], half_sem.at[1], tp(sibling)
    )
    send(half)
    wait_x(sibling)
    add_block(sibling)
    half.wait_recv()
    chip_total = half_send[core] + half_recv[...]
    chip_sum[z] = chip_total.astype(chip_sum.dtype)
    for k in range(1, chips):
        send(
            remote(
                chip_sum.at[z],
                chip_sum.at[z],
                chip_send.at[k],
                chip_recv.at[z],
                tp(at_chip(k) * CORES + core),
            )
        )
    add_same(0)
    arrive(1)
    add_other(0)
    add_same(1)
    for k in range(1, chips):
        v = at_chip(k)
        remote(
            chip_sum.at[z], chip_sum.at[v], chip_send.at[0], chip_recv.at[v], tp(sibling)
        ).wait_recv()
        chip_total = chip_total + chip_sum[v].astype(F32)
    ranks[core] = chip_total.astype(BF16)
    rank_copy = remote(
        ranks.at[core], ranks.at[core], rank_sem.at[0], rank_sem.at[1], tp(sibling)
    )
    send(rank_copy)
    add_other(1)
    remote(
        ranks.at[core], ranks.at[1 - core], rank_sem.at[0], rank_sem.at[1], tp(sibling)
    ).wait_recv()

    def lift(side_rows):
        rank = ranks[side_rows].astype(F32)
        picked = [(rank * mask_of(side_rows, a)).astype(BF16) for a in range(owned)]
        return dot(jnp.concatenate(picked, axis=1), up[...])

    lift_send[...] = lift(other).astype(BF16)
    lift_copy = remote(lift_send, lift_recv, lift_sem.at[0], lift_sem.at[1], peer)
    send(lift_copy)
    lift_own[...] = lift(side)
    for i in range(2, last):
        arrive(i)
        if i == last - 1:
            cache_copy.start()
        add_same(i)
        add_other(i)
    lift_copy.wait_recv()
    span = columns + HEAD
    front = (acc[:, 0:span] + lift_own[...] + lift_recv[...].astype(F32)).astype(BF16)
    key_block = acc[:, span:].astype(BF16)

    def spread(shape, row_axis, col_axis):
        row = iota(shape, row_axis)
        u = row // pad
        i = lax.rem(row, pad)
        step = i // here
        source = step * requests + u * here + lax.rem(i, here)
        return jnp.where(
            (i < STEPS * here) & (iota(shape, col_axis) == source), 1.0, 0.0
        ).astype(BF16)

    place = spread((T * pad, rows), 0, 1)
    heads_send[:, :, 0:span] = dot(place, front).astype(BF16).reshape(T, pad, span)
    heads_send[:, :, span:] = dot(place, key_block).astype(BF16).reshape(T, pad, HEAD)
    for k in range(1, T):
        u = lax.rem(me + k, T)
        send(
            remote(
                heads_send.at[u], heads_recv.at[me], heads_ssem.at[k], heads_rsem.at[me], tp(u)
            )
        )
    heads_recv[me] = heads_send[me]
    for u in wide_order:
        wide_copy(u).start()
    cache_copy.wait()
    for j in range(here):
        pairs[j] = cache[j].reshape(pairs.shape[1], pairs.shape[2])

    row = iota((pad, HEAD), 0)
    lane = iota((pad, HEAD), 1)
    step = row // here
    index = lax.rem(row, here)
    position = jnp.zeros((pad, HEAD), jnp.int32)
    for j in range(here):
        position = jnp.where(index == j, length_ref[j], position)
    position = (position + step).astype(F32)
    freq = jnp.exp(
        -(lax.rem(lane, HEAD // 2).astype(F32) * 2.0 / HEAD) * math.log(500000.0)
    )
    angle = position * freq
    cosine = jnp.cos(angle)
    sine = jnp.where(lane < HEAD // 2, -jnp.sin(angle), jnp.sin(angle))

    def turn(block):
        wide = block.astype(F32)
        return (wide * cosine + pltpu.roll(wide, HEAD // 2, 1) * sine).astype(BF16).astype(F32)

    results[...] = jnp.zeros(results.shape, F32)
    for k in range(1, T):
        u = lax.rem(me + k, T)
        remote(
            heads_send.at[u], heads_recv.at[u], heads_ssem.at[0], heads_rsem.at[u], tp(sibling)
        ).wait_recv()
    new_keys = []
    new_values = []
    for h in range(T):
        for g in range(group):
            turned[h, pl.ds(g * pad, pad), :] = turn(
                heads_recv[h, :, g * HEAD : (g + 1) * HEAD]
            )
        new_values.append(heads_recv[h, :, columns : columns + HEAD].astype(F32))
        new_keys.append(turn(heads_recv[h, :, columns + HEAD :]))

    scale = HEAD ** (-0.5)
    per = STEPS * group
    count = pairs.shape[1]
    for j in range(here):
        queries = []
        scores = []
        fresh = [[] for _ in range(STEPS)]
        for h in range(T):
            query = jnp.concatenate(
                [
                    turned[h, pl.ds(s * here + j, group, stride=pad), :]
                    for s in range(STEPS)
                ],
                axis=0,
            )
            keys = pairs[j, :, h * HEAD : (h + 1) * HEAD]
            scores.append(
                lax.dot_general(
                    query.astype(BF16),
                    keys,
                    (((1,), (1,)), ((), ())),
                    preferred_element_type=F32,
                )
            )
            for s in range(STEPS):
                at = s * here + j
                fresh[s].append(
                    jnp.sum(query * new_keys[h][at : at + 1, :], axis=1, keepdims=True)
                )
        score = jnp.concatenate(scores, axis=0) * scale
        lanes = iota((T * per, count), 1)
        valid = (lanes < 2 * length_ref[j]) & (lax.rem(lanes, 2) == 0)
        score = jnp.where(valid, score, -1e30)
        top = jnp.max(score, axis=1, keepdims=True)
        row_step = lax.rem(iota((T * per, 1), 0), per) // group
        new_scores = []
        for s in range(STEPS):
            new = jnp.concatenate(fresh[s], axis=0) * scale
            new = jnp.where(row_step >= s, new, -1e30)
            new_scores.append(new)
            top = jnp.maximum(top, new)
        old_exp = jnp.exp(score - top)
        total = jnp.sum(old_exp, axis=1, keepdims=True)
        new_exp = [jnp.exp(new - top) for new in new_scores]
        for new in new_exp:
            total = total + new
        inverse = 1.0 / total
        shifted = pltpu.roll(old_exp * inverse, 1, 1).astype(BF16)
        new_weight = [(new * inverse).astype(BF16).astype(F32) for new in new_exp]
        for h in range(T):
            part = slice(h * per, (h + 1) * per)
            result = dot(shifted[part], pairs[j, :, h * HEAD : (h + 1) * HEAD])
            for s in range(STEPS):
                at = s * here + j
                result = result + new_weight[s][part] * new_values[h][at : at + 1, :]
            for s in range(STEPS):
                results[h, pl.ds(s * here + j, group, stride=pad), :] = result[
                    s * group : (s + 1) * group
                ]
    for h in range(T):
        for g in range(group):
            back_send[h, :, g * HEAD : (g + 1) * HEAD] = results[
                h, pl.ds(g * pad, pad), :
            ].astype(BF16)
    for k in range(1, T):
        u = lax.rem(me + k, T)
        send(
            remote(back_send.at[u], back_recv.at[me], back_ssem.at[k], back_rsem.at[me], tp(u))
        )
    back_recv[me] = back_send[me]
    collect = spread((rows, T * pad), 1, 0)
    for k in range(1, T):
        u = lax.rem(me + k, T)
        remote(
            back_send.at[u], back_recv.at[u], back_ssem.at[0], back_rsem.at[u], tp(sibling)
        ).wait_recv()
    attended = dot(collect, back_recv[...].reshape(T * pad, columns)).astype(BF16)

    parts = own_part.shape[1]
    piece = width // parts

    def multiply(i, p):
        lanes = pl.ds(p * piece, piece)
        u = targets[i] * CORES + (1 - core)
        v = targets[i] * CORES + core
        if p == 0:
            wide_copy(u).wait()
            wide_copy(v).wait()
        sib_send[i, p] = dot(attended, wide_out[u, :, lanes]).astype(BF16)
        send(
            remote(
                sib_send.at[i, p],
                sib_recv.at[i, p],
                sib_ssem.at[i, p],
                sib_rsem.at[i, p],
                tp(sibling),
            )
        )
        own_part[i, p] = dot(attended, wide_out[v, :, lanes])

    def take(i, v, p, way, condition):
        @pl.when(condition)
        def _():
            remote(
                sum_send.at[i, p],
                sum_recv.at[way, v, p],
                sum_ssem.at[i, p],
                sum_rsem.at[way, v, p],
                tp(sibling),
            ).wait_recv()
            own_part[i, p] += sum_recv[way, v, p].astype(F32)

    def finish(i, p):
        remote(
            sib_send.at[i, p], sib_recv.at[i, p], sib_ssem.at[i, p], sib_rsem.at[i, p], tp(sibling)
        ).wait_recv()
        own_part[i, p] += sib_recv[i, p].astype(F32)
        v = targets[i]
        if i == last:
            take(i, v, p, 0, z > 0)
            take(i, v, p, 1, z < last)
            return
        take(i, v, p, 0, (v > z) & (z > 0))
        take(i, v, p, 1, (v < z) & (z < last))
        sum_send[i, p] = own_part[i, p].astype(BF16)
        way = jnp.where(v > z, 0, 1)
        send(
            remote(
                sum_send.at[i, p],
                sum_recv.at[way, v, p],
                sum_ssem.at[i, p],
                sum_rsem.at[way, v, p],
                tp(me + jnp.where(v > z, CORES, -CORES)),
            )
        )

    items = [(i, p) for i in range(chips) for p in range(parts)]
    ahead = 1
    for item in items[:ahead]:
        multiply(*item)
    for n, item in enumerate(items):
        if n + ahead < len(items):
            multiply(*items[n + ahead])
        finish(*item)
    mixed = token + jnp.concatenate([own_part[last, p] for p in range(parts)], axis=1)
    for s in range(STEPS):
        out_ref[s] = mixed[s * requests : (s + 1) * requests].astype(BF16)
    for copy in sends:
        copy.wait_send()
    for condition, copy in maybe:
        pl.when(condition)(copy.wait_send)


def fused(
    tokens,
    input_norm_gain,
    query_weight,
    key_weight,
    value_weight,
    output_weight,
    adapter_down_maps,
    adapter_query_up,
    adapter_value_up,
    key_value_cache,
    cached_length,
    request_adapter_entry,
    group_adapter_ids,
    adapter_slot_table,
):
    T = lax.axis_size("tp")
    chips = T // CORES
    requests = tokens.shape[1]
    rows = STEPS * requests
    width = tokens.shape[2]
    here = cached_length.shape[0]
    owned = adapter_down_maps.shape[0]
    columns = query_weight.shape[1]
    group = columns // HEAD
    span = columns + HEAD
    pad = 16
    count = 2 * key_value_cache.shape[1]
    sizes = (T, requests, here, owned, group_adapter_ids.shape[1])
    whole = pl.BlockSpec(memory_space=pltpu.VMEM)
    scalar = pl.BlockSpec(memory_space=pltpu.SMEM)
    left = pl.BlockSpec(memory_space=pl.ANY)
    dma = pltpu.SemaphoreType.DMA
    vmem = pltpu.VMEM
    return pl.pallas_call(
        functools.partial(block_kernel, sizes),
        out_shape=jax.ShapeDtypeStruct(tokens.shape, BF16),
        in_specs=[whole] * 3 + [scalar] * 3 + [left] * 8,
        out_specs=whole,
        scratch_shapes=[
            vmem((T * width, span + HEAD), BF16),
            vmem((T, columns, width), BF16),
            vmem((width, owned * HEAD), BF16),
            vmem((owned * HEAD, span), BF16),
            vmem(key_value_cache.shape, BF16),
            vmem((here, count, KV_HEADS * HEAD), BF16),
            vmem((T, rows, width), BF16),
            vmem((2, rows, width), BF16),
            vmem((2, rows, HEAD), BF16),
            vmem((T, 16, HEAD), BF16),
            vmem((2, 8, HEAD), F32),
            vmem((rows, span + HEAD), F32),
            vmem((2, rows, HEAD), F32),
            vmem((rows, HEAD), F32),
            vmem((chips, rows, HEAD), F32),
            vmem((2, rows, HEAD), BF16),
            vmem((rows, span), F32),
            vmem((rows, span), BF16),
            vmem((rows, span), BF16),
            vmem((T, pad, span + HEAD), BF16),
            vmem((T, pad, span + HEAD), BF16),
            vmem((T, group * pad, HEAD), F32),
            vmem((T, group * pad, HEAD), F32),
            vmem((T, pad, columns), BF16),
            vmem((T, pad, columns), BF16),
            vmem((chips, 2, rows, width // 2), F32),
            vmem((chips, 2, rows, width // 2), BF16),
            vmem((chips, 2, rows, width // 2), BF16),
            vmem((chips, 2, rows, width // 2), BF16),
            vmem((2, chips, 2, rows, width // 2), BF16),
            dma((3, T)),
            dma((T,)),
            dma((3, owned)),
            dma(()),
            dma(()),
            dma((T,)),
            dma((chips, 2)),
            dma((chips,)),
            dma((3,)),
            dma((3,)),
            dma((T,)),
            dma((T,)),
            dma((2,)),
            dma((chips,)),
            dma((chips,)),
            dma((2,)),
            dma((2,)),
            dma((T,)),
            dma((T,)),
            dma((T,)),
            dma((T,)),
            dma((chips, 2)),
            dma((chips, 2)),
            dma((chips, 2)),
            dma((2, chips, 2)),
        ],
        compiler_params=pltpu.CompilerParams(
            collective_id=0, has_side_effects=True, vmem_limit_bytes=56 * 1024 * 1024
        ),
    )(
        tokens,
        input_norm_gain,
        request_adapter_entry.reshape(1, requests),
        group_adapter_ids,
        adapter_slot_table,
        cached_length,
        query_weight,
        key_weight,
        value_weight,
        output_weight,
        adapter_down_maps,
        adapter_query_up,
        adapter_value_up,
        key_value_cache,
    )


def device_program(*arrays):
    tokens, query_weight, key_weight, down = arrays[0], arrays[2], arrays[3], arrays[6]
    T = lax.axis_size("tp")
    whole_heads = (
        key_weight.shape[1] == HEAD
        and T == KV_HEADS
        and lax.axis_size("srv") == 2
        and down.shape[2] == HEAD
        and tokens.shape[2] == query_weight.shape[1]
        and tokens.shape[2] <= 13 * HEAD
        and (STEPS * tokens.shape[1]) % 16 == 0
        and STEPS * tokens.shape[1] <= HEAD
    )
    return fused(*arrays) if whole_heads else on_device(*arrays)


def solution(mesh):
    placed = (
        P(None, ("rep", "srv"), "tp"),
        P("tp"),
        P(None, "tp"),
        P(None, "tp"),
        P(None, "tp"),
        P("tp", None),
        P("srv", "tp", None),
        P("srv", None, "tp"),
        P("srv", None, "tp"),
        P(("rep", "srv", "tp"), None, None, None),
        P(("rep", "srv", "tp")),
        P(("rep", "srv")),
        P(),
        P(),
    )
    return jax.shard_map(
        device_program,
        mesh=mesh,
        in_specs=placed,
        out_specs=P(None, ("rep", "srv"), "tp"),
        check_vma=False,
    )
```
